128 devices in a mesh: energy: 16 (over x_lo, y, core), layer: 8 (over z, x_hi).
Axes of the slice: x: 4 (x_hi: 2, x_lo: 2; x = x_hi * 2 + x_lo), y: 4, z: 4, core: 2. Of those that a mesh axis runs over, the one named last changes fastest.
Arguments:
- green: bfloat16 [512, 8, 256, 256], P('energy', 'layer'), may hold values from -6 to 6
- gradient: bfloat16 [8, 256, 256], P('layer'), may hold values from -0.375 to 0.375
- left_coupling: bfloat16 [8, 256, 128], P('layer'), may hold values from -0.5 to 0.5
- right_coupling: bfloat16 [8, 256, 128], P('layer'), may hold values from -0.5 to 0.5
- dynamical: float32 [8, 256, 256], P('layer'), may hold values from -0.2 to 3
- omega_sq: float32 [16], replicated, may hold values from 1 to 4
- shifts: int32 [16], replicated, may hold values from 1 to 32, as said below
Outputs:
- phonon_self: float32 [16, 8, 256, 256], P('energy', 'layer')
- phonon_green: float32 [16, 8, 256, 256], P('energy', 'layer')
- electron_self: bfloat16 [512, 8, 256, 256], P('energy', 'layer')
The draws below stay inside these ranges and needn't reach their ends.
Inputs may be any that keep to these rules, and one draw needn't show every extreme that they name: `shifts`: the largest shift is 32.
All inputs are finite; a program needn't handle non-finite values.
Results may differ from the reference program's by a relative error of at most 0.017.
Values may be sent and summed in bfloat16 or wider, within the bound.
A program may use at most 192 MiB of HBM per device.

```python
import math
import jax
import jax.numpy as jnp
from jax import lax

NB = 256
BND = 128
E_DEV = 32
NEWTON = 3
NE = 512
LAYERS = 8
W = 16


def draw_dynamical(key, part):
    halves = jax.random.split(key, 2)
    log_diag = jax.random.uniform(halves[0], (LAYERS, NB), jnp.float32, 0.0, math.log(3.0))
    diagonal = jnp.exp(log_diag)
    spread = jnp.clip(0.03 * jax.random.normal(halves[1], (LAYERS, NB, NB), jnp.float32), -0.2, 0.2)
    identity = jnp.eye(NB, dtype=jnp.float32)
    return spread * (1.0 - identity) + diagonal[:, :, None] * identity


def draw_shifts(key, part):
    values = jax.random.randint(key, (W,), 1, E_DEV + 1)
    position = jax.random.randint(jax.random.fold_in(key, 7), (), 0, W)
    return values.at[position].set(E_DEV).astype(jnp.int32)


def shard_levels(stream_key, extent, cuts, low, largest):
    def one(dim, parts):
        draws = jax.random.uniform(jax.random.fold_in(jax.random.fold_in(stream_key, 6), dim), (parts,), jnp.float32, low / len(cuts), largest / len(cuts))
        return jnp.repeat(jnp.exp(draws), extent[dim] // parts).reshape((-1,) + (1,) * (len(extent) - dim - 1))

    factor_of = one(*cuts[0])
    for cut in cuts[1:]:
        factor_of = factor_of * one(*cut)
    return factor_of


def centred(stream_key, dims, scale, bound, shards=(), kind=jnp.bfloat16):
    entries = jax.random.normal(stream_key, dims, jnp.float32) * scale
    if len(shards) > 0:
        entries = shard_levels(stream_key, dims, shards, -0.22, 0.18) * entries
    return jnp.clip(entries, min=-bound, max=bound).astype(kind)


def setup_inputs(seed: int = 0) -> dict:
    key_of = jax.random.split(jax.random.key(seed), 8)
    green = centred(key_of[0], (NE, LAYERS, NB, NB), 1.0, 6.0, ((0, 16), (1, 8)))
    gradient = centred(key_of[1], (LAYERS, NB, NB), NB ** -0.5, 0.375, ((0, 8),))
    left_coupling = centred(key_of[2], (LAYERS, NB, BND), BND ** -0.5, 0.5, ((0, 8),))
    right_coupling = centred(key_of[3], (LAYERS, NB, BND), BND ** -0.5, 0.5, ((0, 8),))
    dynamical = draw_dynamical(jax.random.fold_in(key_of[7], 71), 0)
    omega_sq = jnp.clip(jnp.exp(jax.random.uniform(key_of[5], (W,), jnp.float32, math.log(1.0), math.log(4.0))), 1.0, 4.0)
    shifts = draw_shifts(jax.random.fold_in(key_of[7], 71), 0)
    return {"green": green, "gradient": gradient, "left_coupling": left_coupling, "right_coupling": right_coupling, "dynamical": dynamical, "omega_sq": omega_sq, "shifts": shifts}


coupling = 0.01

def invert(matrix):
    identity = jnp.eye(matrix.shape[-1], dtype=jnp.float32)
    diagonal = jnp.diagonal(matrix, axis1=1, axis2=2)
    approx = identity[None] / diagonal[:, None, :]
    for repeat in range(NEWTON):
        product = jnp.einsum('kij,kjl->kil', matrix, approx, precision=lax.Precision.HIGHEST)
        approx = 2.0 * approx - jnp.einsum('kij,kjl->kil', approx, product, precision=lax.Precision.HIGHEST)
    return approx

def reference(green, gradient, left_coupling, right_coupling, dynamical, omega_sq, shifts):
    zero_blocks = jnp.zeros((NE, 1, BND, BND), jnp.bfloat16)
    from_left = jnp.concatenate([zero_blocks, green[:, :-1, NB - BND:, NB - BND:]], axis=1)
    from_right = jnp.concatenate([green[:, 1:, :BND, :BND], zero_blocks], axis=1)
    energies = jnp.arange(NE, dtype=jnp.int32)
    scale = 1.0 / math.sqrt(NE)

    def one_layer(inputs):
        blocks, layer_grad, left_cpl, right_cpl, left_in, right_in, stiffness = inputs
        grad_wide = layer_grad.astype(jnp.float32)
        first_half = jnp.einsum('ij,ejk->eik', grad_wide, blocks.astype(jnp.float32)).astype(jnp.bfloat16)
        summed = jnp.einsum('eij,kj->eik', first_half.astype(jnp.float32), grad_wide)
        left_part = jnp.einsum('ij,ejk->eik', left_cpl.astype(jnp.float32), left_in.astype(jnp.float32)).astype(jnp.bfloat16)
        summed = summed + jnp.einsum('eij,kj->eik', left_part.astype(jnp.float32), left_cpl.astype(jnp.float32))
        right_part = jnp.einsum('ij,ejk->eik', right_cpl.astype(jnp.float32), right_in.astype(jnp.float32)).astype(jnp.bfloat16)
        summed = summed + jnp.einsum('eij,kj->eik', right_part.astype(jnp.float32), right_cpl.astype(jnp.float32))
        sandwich = summed.astype(jnp.bfloat16)
        sandwich_wide = sandwich.astype(jnp.float32)

        def phonon_term(offset):
            upward = energies + offset
            inside = (upward < NE).astype(jnp.float32)
            slices = blocks[jnp.minimum(upward, NE - 1)].astype(jnp.float32) * inside[:, None, None]
            return lax.optimization_barrier(jnp.sum(sandwich_wide * slices, axis=0)) * scale
        phonon_self = lax.map(phonon_term, shifts)
        identity = jnp.eye(NB, dtype=jnp.float32)
        matrix = stiffness[None] + omega_sq[:, None, None] * identity[None] + coupling * phonon_self
        phonon_green = invert(matrix)
        rounded = phonon_green.astype(jnp.bfloat16)

        def add_term(running, paired):
            green_one, offset = paired
            downward = energies - offset
            inside = (downward >= 0).astype(jnp.float32)
            slices = sandwich_wide[jnp.maximum(downward, 0)] * inside[:, None, None]
            return (running + green_one.astype(jnp.float32)[None] * slices, None)
        mixture, unused = lax.scan(add_term, jnp.zeros((NE, NB, NB), jnp.float32), (rounded, shifts))
        mixture = mixture.astype(jnp.bfloat16)
        second = jnp.einsum('ij,ejk->eik', grad_wide, mixture.astype(jnp.float32)).astype(jnp.bfloat16)
        electron = jnp.einsum('eij,kj->eik', second.astype(jnp.float32), grad_wide).astype(jnp.bfloat16)
        return (phonon_self, phonon_green, electron)
    layered = (jnp.moveaxis(green, 1, 0), gradient, left_coupling, right_coupling, jnp.moveaxis(from_left, 1, 0), jnp.moveaxis(from_right, 1, 0), dynamical)
    self_all, green_all, electron_all = lax.map(one_layer, layered)
    return (jnp.moveaxis(self_all, 0, 1), jnp.moveaxis(green_all, 0, 1), jnp.moveaxis(electron_all, 0, 1))
```

```python
import functools
import math

import jax
import jax.numpy as jnp
from jax import lax
from jax.experimental import pallas as pl
from jax.experimental.pallas import tpu as pltpu
from jax.sharding import PartitionSpec as P

NEWTON = 3
COUPLING = 0.01
MESH = pl.DeviceIdType.MESH
BF = jnp.bfloat16
F32 = jnp.float32

PER = 32
NB = 256
HALF = 128
CH = 4
STEPS = PER // CH
AHEAD = 2
W = 16
CHIPS = 8
ROWS = 32


def nn(a, b, **kw):
    return lax.dot_general(a, b, (((1,), (0,)), ((), ())), preferred_element_type=F32, **kw)


def nt(a, b, **kw):
    return lax.dot_general(a, b, (((1,), (1,)), ((), ())), preferred_element_type=F32, **kw)


def tree(terms):
    while len(terms) > 1:
        terms = [terms[i] + terms[i + 1] if i + 1 < len(terms) else terms[i] for i in range(0, len(terms), 2)]
    return terms[0]


def scatter_kernel(
    scale, shifts, omega, green, grad, left_cpl, right_cpl, stiff,
    self_out, green_out, turned_out,
    gpad, win, left_in, right_in, first, acc, part, sums, from_core, from_chip, rounded, mix, tile, turned,
    g_sem, ls, lr, rs, rr, us, ur, c1s, c1r, c2s, c2r, gs, gr, fs, fr, ts,
):
    me = lax.axis_index("energy")
    layer = lax.axis_index("layer")
    core = lax.rem(me, 2)
    chip = me // 2
    has_lower, has_upper = me > 0, me < 15
    has_left, has_right = layer > 0, layer < 7
    partner = {"energy": me + 1 - 2 * core, "layer": layer}

    def g_copy(c):
        return pltpu.make_async_copy(
            green.at[pl.ds(c * CH, CH)], gpad.at[pl.ds(PER + c * CH, CH)], g_sem.at[c])

    def left_copy(c):
        return pltpu.make_async_remote_copy(
            src_ref=green.at[pl.ds(c * CH, CH), pl.ds(HALF, HALF), pl.ds(HALF, HALF)],
            dst_ref=left_in.at[pl.ds(c * CH, CH)], send_sem=ls.at[c], recv_sem=lr.at[c],
            device_id={"energy": me, "layer": lax.rem(layer + 1, 8)}, device_id_type=MESH)

    def right_copy(c):
        return pltpu.make_async_remote_copy(
            src_ref=green.at[pl.ds(c * CH, CH), pl.ds(0, HALF), pl.ds(0, HALF)],
            dst_ref=right_in.at[pl.ds(c * CH, CH)], send_sem=rs.at[c], recv_sem=rr.at[c],
            device_id={"energy": me, "layer": lax.rem(layer + 7, 8)}, device_id_type=MESH)

    def up_copy(c):
        return pltpu.make_async_remote_copy(
            src_ref=win.at[pl.ds(PER + c * CH, CH)], dst_ref=win.at[pl.ds(c * CH, CH)],
            send_sem=us.at[c], recv_sem=ur.at[c],
            device_id={"energy": lax.rem(me + 1, 16), "layer": layer}, device_id_type=MESH)

    def start_surfaces(c):
        @pl.when(has_right)
        def _():
            left_copy(c).start()

        @pl.when(has_left)
        def _():
            right_copy(c).start()

    for c in range(STEPS):
        g_copy(c).start()

    barrier = pltpu.get_barrier_semaphore()
    for k in range(1, 16):
        pl.semaphore_signal(
            barrier, inc=1, device_id={"energy": lax.rem(me + k, 16), "layer": layer}, device_id_type=MESH)

    @pl.when(has_right)
    def _():
        pl.semaphore_signal(barrier, inc=1, device_id={"energy": me, "layer": layer + 1}, device_id_type=MESH)

    @pl.when(has_left)
    def _():
        pl.semaphore_signal(barrier, inc=1, device_id={"energy": me, "layer": layer - 1}, device_id_type=MESH)

    pl.semaphore_wait(barrier, 15 + has_left.astype(jnp.int32) + has_right.astype(jnp.int32))

    for c in range(AHEAD):
        start_surfaces(c)

    def clear(i, carry):
        zero = jnp.zeros((NB, NB), BF)
        gpad[i] = zero
        gpad[2 * PER + i] = zero
        return carry

    lax.fori_loop(0, PER, clear, 0)

    @pl.when(jnp.logical_not(has_lower))
    def _():
        def fill(i, carry):
            win[i] = jnp.zeros((NB, NB), BF)
            return carry

        lax.fori_loop(0, PER, fill, 0)

    @pl.when(jnp.logical_not(has_left))
    def _():
        def fill(i, carry):
            left_in[i] = jnp.zeros((HALF, HALF), BF)
            return carry

        lax.fori_loop(0, PER, fill, 0)

    @pl.when(jnp.logical_not(has_right))
    def _():
        def fill(i, carry):
            right_in[i] = jnp.zeros((HALF, HALF), BF)
            return carry

        lax.fori_loop(0, PER, fill, 0)

    def clear_acc(w, carry):
        acc[w] = jnp.zeros((NB, NB), F32)
        return carry

    lax.fori_loop(0, W, clear_acc, 0)

    for c in range(STEPS):
        g_copy(c).wait()

    def correlate(s_base, g_base):
        def one(t, carry):
            rows = pl.ds(pl.multiple_of(t * ROWS, ROWS), ROWS)
            held = [win[s_base + i, rows, :] for i in range(CH)]
            for w in range(W):
                at = g_base + shifts[w]
                terms = [held[i] * gpad[at + i, rows, :] for i in range(CH)]
                acc[w, rows, :] += tree(terms).astype(F32)
            return carry

        lax.fori_loop(0, NB // ROWS, one, 0)

    a = grad[...]
    lc = left_cpl[...]
    rc = right_cpl[...]

    def step(c, carry):
        e0 = c * CH
        for i in range(CH):
            first[pl.ds(i * NB, NB), :] = nn(a, gpad[PER + e0 + i]).astype(BF)

        @pl.when(has_left)
        def _():
            left_copy(c).wait_recv()

        @pl.when(has_right)
        def _():
            right_copy(c).wait_recv()

        lp = [nn(lc, left_in[e0 + i]).astype(BF) for i in range(CH)]
        rp = [nn(rc, right_in[e0 + i]).astype(BF) for i in range(CH)]
        for i in range(CH):
            total = nt(first[pl.ds(i * NB, NB), :], a) + nt(lp[i], lc) + nt(rp[i], rc)
            win[PER + e0 + i] = total.astype(BF)

        @pl.when(has_upper)
        def _():
            up_copy(c).start()

        @pl.when(has_right)
        def _():
            left_copy(c).wait_send()

        @pl.when(has_left)
        def _():
            right_copy(c).wait_send()

        @pl.when(c + AHEAD < STEPS)
        def _():
            start_surfaces(c + AHEAD)

        correlate(PER + e0, PER + e0)

        @pl.when(c > 0)
        def _():
            @pl.when(has_lower)
            def _():
                up_copy(c - 1).wait_recv()

            correlate(e0 - CH, e0 - CH)

        return carry

    lax.fori_loop(0, STEPS, step, 0)

    def core_copy(j):
        return pltpu.make_async_remote_copy(
            src_ref=part.at[j], dst_ref=from_core.at[j], send_sem=c1s.at[j], recv_sem=c1r.at[j],
            device_id=partner, device_id_type=MESH)

    last = PER - CH

    @pl.when(has_lower)
    def _():
        up_copy(STEPS - 1).wait_recv()

    def finish(w, store):
        at = last + shifts[w]

        def one(t, carry):
            rows = pl.ds(pl.multiple_of(t * ROWS, ROWS), ROWS)
            terms = [win[last + i, rows, :] * gpad[at + i, rows, :] for i in range(CH)]
            store(rows, (acc[w, rows, :] + tree(terms).astype(F32)) * scale)
            return carry

        lax.fori_loop(0, NB // ROWS, one, 0)

    def theirs(k, carry):
        j = lax.rem(chip + k, CHIPS)

        def store(rows, value):
            part[j, rows, :] = value.astype(BF)

        finish(2 * j + 1 - core, store)
        core_copy(j).start()
        return carry

    lax.fori_loop(1, CHIPS + 1, theirs, 0)

    def ours(k, carry):
        j = lax.rem(chip + k, CHIPS)
        w = 2 * j + core

        def store(rows, value):
            acc[w, rows, :] = value

        finish(w, store)
        return carry

    lax.fori_loop(1, CHIPS + 1, ours, 0)

    def chip_copy(k):
        return pltpu.make_async_remote_copy(
            src_ref=sums.at[k - 1], dst_ref=from_chip.at[k - 1], send_sem=c2s.at[k - 1], recv_sem=c2r.at[k - 1],
            device_id={"energy": 2 * lax.rem(chip + k, CHIPS) + core, "layer": layer}, device_id_type=MESH)

    def join(k, carry):
        j = lax.rem(chip + k, CHIPS)
        w = 2 * j + core
        core_copy(j).wait_recv()

        def one(t, c2):
            rows = pl.ds(pl.multiple_of(t * ROWS, ROWS), ROWS)
            sums[k - 1, rows, :] = (acc[w, rows, :] + from_core[j, rows, :].astype(F32)).astype(BF)
            return c2

        lax.fori_loop(0, NB // ROWS, one, 0)
        chip_copy(k).start()
        return carry

    lax.fori_loop(1, CHIPS, join, 0)
    core_copy(chip).wait_recv()
    for k in range(1, CHIPS):
        chip_copy(k).wait_recv()

    def total_rows(t, carry):
        rows = pl.ds(pl.multiple_of(t * ROWS, ROWS), ROWS)
        value = acc[me, rows, :] + from_core[chip, rows, :].astype(F32)
        for k in range(CHIPS - 1):
            value = value + from_chip[k, rows, :].astype(F32)
        self_out[rows, :] = value
        return carry

    lax.fori_loop(0, NB // ROWS, total_rows, 0)

    on_diag = lax.broadcasted_iota(jnp.int32, (NB, NB), 0) == lax.broadcasted_iota(jnp.int32, (NB, NB), 1)
    matrix = stiff[...] + COUPLING * self_out[...]
    matrix = matrix + jnp.where(on_diag, omega[me], 0.0)
    diag = jnp.where(on_diag, matrix, 0.0)
    inv_row = 1.0 / jnp.sum(diag, axis=0, keepdims=True)
    inv_col = 1.0 / jnp.sum(diag, axis=1, keepdims=True)
    approx = jnp.where(on_diag, 2.0 * inv_col, 0.0) - inv_col * (matrix * inv_row)
    for _ in range(NEWTON - 1):
        product = nn(matrix, approx, precision=lax.Precision.HIGHEST)
        approx = 2.0 * approx - nn(approx, product, precision=lax.Precision.HIGHEST)
    green_out[...] = approx
    rounded[me] = approx.astype(BF)

    def gather_copy(k):
        return pltpu.make_async_remote_copy(
            src_ref=rounded.at[me], dst_ref=rounded.at[me], send_sem=gs.at[k - 1], recv_sem=gr.at[k - 1],
            device_id={"energy": 2 * lax.rem(chip + k, CHIPS) + core, "layer": layer}, device_id_type=MESH)

    def gather_arrival(k):
        w = 2 * lax.rem(chip + CHIPS - k, CHIPS) + core
        return pltpu.make_async_remote_copy(
            src_ref=rounded.at[w], dst_ref=rounded.at[w], send_sem=gs.at[k - 1], recv_sem=gr.at[k - 1],
            device_id={"energy": w, "layer": layer}, device_id_type=MESH)

    def pass_on(k, whose):
        w = 2 * lax.rem(chip + CHIPS - k, CHIPS) + whose
        return pltpu.make_async_remote_copy(
            src_ref=rounded.at[w], dst_ref=rounded.at[w], send_sem=fs.at[k], recv_sem=fr.at[k],
            device_id=partner, device_id_type=MESH)

    pass_on(0, core).start()
    for k in range(1, CHIPS):
        gather_copy(k).start()

    group = 4
    for g in range(W // group):
        ws = []
        for k in (2 * g, 2 * g + 1):
            if k > 0:
                gather_arrival(k).wait_recv()
                pass_on(k, core).start()
        for k in (2 * g, 2 * g + 1):
            pass_on(k, 1 - core).wait_recv()
            owner = 2 * lax.rem(chip + CHIPS - k, CHIPS)
            ws += [owner, owner + 1]
        final = g == W // group - 1

        def mix_rows(t, carry):
            rows = pl.ds(pl.multiple_of(t * ROWS, ROWS), ROWS)
            held = [rounded[w, rows, :] for w in ws]
            ats = [PER - shifts[w] for w in ws]
            for e in range(PER):
                terms = [held[i] * win[ats[i] + e, rows, :] for i in range(group)]
                value = tree(terms).astype(F32)
                if g > 0:
                    value = mix[e, rows, :] + value
                if final:
                    tile[pl.ds(e * ROWS, ROWS), :] = value.astype(BF)
                else:
                    mix[e, rows, :] = value
            if final:
                out = nt(tile[...], a).astype(BF)
                for e in range(PER):
                    turned[e, rows, :] = out[e * ROWS:(e + 1) * ROWS]
                turn_copy(t).start()
            return carry

        def turn_copy(t):
            rows = pl.ds(pl.multiple_of(t * ROWS, ROWS), ROWS)
            return pltpu.make_async_copy(turned.at[:, rows, :], turned_out.at[:, rows, :], ts.at[t])

        lax.fori_loop(0, NB // ROWS, mix_rows, 0)

    for t in range(NB // ROWS):
        turn_copy(t).wait()
    for c in range(STEPS):
        @pl.when(has_upper)
        def _():
            up_copy(c).wait_send()
    for j in range(CHIPS):
        core_copy(j).wait_send()
        pass_on(j, core).wait_send()
    for k in range(1, CHIPS):
        chip_copy(k).wait_send()
        gather_copy(k).wait_send()


def last_kernel(grad, turned, out):
    a = grad[...]
    for i in range(out.shape[0]):
        out[i] = nn(a, turned[i]).astype(BF)


def body(green, gradient, left_coupling, right_coupling, dynamical, omega_sq, shifts):
    scale = 1.0 / math.sqrt(PER * lax.axis_size("energy"))
    vmem = pl.BlockSpec(memory_space=pltpu.VMEM)
    smem = pl.BlockSpec(memory_space=pltpu.SMEM)
    hbm = pl.BlockSpec(memory_space=pl.ANY)
    dma = pltpu.SemaphoreType.DMA
    own_self, own_green, turned = pl.pallas_call(
        functools.partial(scatter_kernel, scale),
        out_shape=[
            jax.ShapeDtypeStruct((NB, NB), F32),
            jax.ShapeDtypeStruct((NB, NB), F32),
            jax.ShapeDtypeStruct((PER, NB, NB), BF),
        ],
        in_specs=[smem, smem, hbm, vmem, vmem, vmem, vmem],
        out_specs=[vmem, vmem, hbm],
        scratch_shapes=[
            pltpu.VMEM((3 * PER, NB, NB), BF),
            pltpu.VMEM((2 * PER, NB, NB), BF),
            pltpu.VMEM((PER, HALF, HALF), BF),
            pltpu.VMEM((PER, HALF, HALF), BF),
            pltpu.VMEM((CH * NB, NB), BF),
            pltpu.VMEM((W, NB, NB), F32),
            pltpu.VMEM((CHIPS, NB, NB), BF),
            pltpu.VMEM((CHIPS - 1, NB, NB), BF),
            pltpu.VMEM((CHIPS, NB, NB), BF),
            pltpu.VMEM((CHIPS - 1, NB, NB), BF),
            pltpu.VMEM((W, NB, NB), BF),
            pltpu.VMEM((PER, NB, NB), F32),
            pltpu.VMEM((PER * ROWS, NB), BF),
            pltpu.VMEM((PER, NB, NB), BF),
            dma((STEPS,)),
            dma((STEPS,)), dma((STEPS,)), dma((STEPS,)), dma((STEPS,)), dma((STEPS,)), dma((STEPS,)),
            dma((CHIPS,)), dma((CHIPS,)), dma((CHIPS - 1,)), dma((CHIPS - 1,)),
            dma((CHIPS - 1,)), dma((CHIPS - 1,)), dma((CHIPS,)), dma((CHIPS,)),
            dma((NB // ROWS,)),
        ],
        compiler_params=pltpu.CompilerParams(
            collective_id=0, has_side_effects=True, vmem_limit_bytes=58 << 20),
        name="scatter",
    )(shifts, omega_sq, green[:, 0], gradient[0], left_coupling[0], right_coupling[0], dynamical[0])
    block = pl.BlockSpec((4, NB, NB), lambda i: (i, 0, 0))
    electron = pl.pallas_call(
        last_kernel,
        grid=(PER // 4,),
        in_specs=[pl.BlockSpec((NB, NB), lambda i: (0, 0)), block],
        out_specs=block,
        out_shape=jax.ShapeDtypeStruct((PER, NB, NB), BF),
        name="last",
    )(gradient[0], turned)
    return own_self[None, None], own_green[None, None], electron[:, None]


def solution(mesh):
    return jax.shard_map(
        body,
        mesh=mesh,
        in_specs=(
            P("energy", "layer", None, None),
            P("layer", None, None),
            P("layer", None, None),
            P("layer", None, None),
            P("layer", None, None),
            P(),
            P(),
        ),
        out_specs=(
            P("energy", "layer", None, None),
            P("energy", "layer", None, None),
            P("energy", "layer", None, None),
        ),
        check_vma=False,
    )
```

```python
import functools
import math

import jax
import jax.numpy as jnp
from jax import lax
from jax.experimental import pallas as pl
from jax.experimental.pallas import tpu as pltpu
from jax.sharding import PartitionSpec as P

NEWTON = 3
COUPLING = 0.01
MESH = pl.DeviceIdType.MESH
BF = jnp.bfloat16
F32 = jnp.float32

PER = 32
NB = 256
HALF = 128
CH = 2
STEPS = PER // CH
AHEAD = 4
LAG = 4
W = 16
CHIPS = 8
LAST = 16
ROWS = 32


def nn(a, b, **kw):
    return lax.dot_general(a, b, (((1,), (0,)), ((), ())), preferred_element_type=F32, **kw)


def nt(a, b, **kw):
    return lax.dot_general(a, b, (((1,), (1,)), ((), ())), preferred_element_type=F32, **kw)


def tree(terms):
    while len(terms) > 1:
        terms = [terms[i] + terms[i + 1] if i + 1 < len(terms) else terms[i] for i in range(0, len(terms), 2)]
    return terms[0]


def scatter_kernel(
    scale, shifts, omega, green, grad, left_cpl, right_cpl, stiff,
    self_out, green_out, turned_out,
    gpad, win, left_in, right_in, first, acc, part, sums, from_core, from_chip, rounded, mix, tile, turned, held_over,
    g_sem, ls, lr, rs, rr, us, ur, c1s, c1r, c2s, c2r, gs, gr, fs, fr, ts, hs, hr,
):
    me = lax.axis_index("energy")
    layer = lax.axis_index("layer")
    core = lax.rem(me, 2)
    chip = me // 2
    has_lower, has_upper = me > 0, me < 15
    has_left, has_right = layer > 0, layer < 7
    partner = {"energy": me + 1 - 2 * core, "layer": layer}

    def g_copy(c):
        return pltpu.make_async_copy(
            green.at[pl.ds(c * CH, CH)], gpad.at[pl.ds(PER + c * CH, CH)], g_sem.at[c])

    def left_copy(c):
        return pltpu.make_async_remote_copy(
            src_ref=green.at[pl.ds(c * CH, CH), pl.ds(HALF, HALF), pl.ds(HALF, HALF)],
            dst_ref=left_in.at[pl.ds(c * CH, CH)], send_sem=ls.at[c], recv_sem=lr.at[c],
            device_id={"energy": me, "layer": lax.rem(layer + 1, 8)}, device_id_type=MESH)

    def right_copy(c):
        return pltpu.make_async_remote_copy(
            src_ref=green.at[pl.ds(c * CH, CH), pl.ds(0, HALF), pl.ds(0, HALF)],
            dst_ref=right_in.at[pl.ds(c * CH, CH)], send_sem=rs.at[c], recv_sem=rr.at[c],
            device_id={"energy": me, "layer": lax.rem(layer + 7, 8)}, device_id_type=MESH)

    def up_copy(c):
        return pltpu.make_async_remote_copy(
            src_ref=win.at[pl.ds(PER + c * CH, CH)], dst_ref=win.at[pl.ds(c * CH, CH)],
            send_sem=us.at[c], recv_sem=ur.at[c],
            device_id={"energy": lax.rem(me + 1, 16), "layer": layer}, device_id_type=MESH)

    crossing = 7

    def relay_of(c):
        return lax.rem(4 * lax.rem(c, 4), 6)

    def relayed(c):
        return lax.rem(c, 4) < 3

    def aside_copy(c):
        return pltpu.make_async_remote_copy(
            src_ref=win.at[pl.ds(PER + c * CH, CH)], dst_ref=held_over.at[pl.ds(c // 4 * CH, CH)],
            send_sem=us.at[c], recv_sem=hr.at[c // 4],
            device_id={"energy": relay_of(c), "layer": layer}, device_id_type=MESH)

    def relay_copy(c):
        return pltpu.make_async_remote_copy(
            src_ref=held_over.at[pl.ds(c // 4 * CH, CH)], dst_ref=win.at[pl.ds(c * CH, CH)],
            send_sem=hs.at[c // 4], recv_sem=ur.at[c],
            device_id={"energy": crossing + 1, "layer": layer}, device_id_type=MESH)

    def start_surfaces(c):
        @pl.when(has_right)
        def _():
            left_copy(c).start()

        @pl.when(has_left)
        def _():
            right_copy(c).start()

    for c in range(STEPS):
        g_copy(c).start()

    barrier = pltpu.get_barrier_semaphore()
    for k in range(1, 16):
        pl.semaphore_signal(
            barrier, inc=1, device_id={"energy": lax.rem(me + k, 16), "layer": layer}, device_id_type=MESH)

    @pl.when(has_right)
    def _():
        pl.semaphore_signal(barrier, inc=1, device_id={"energy": me, "layer": layer + 1}, device_id_type=MESH)

    @pl.when(has_left)
    def _():
        pl.semaphore_signal(barrier, inc=1, device_id={"energy": me, "layer": layer - 1}, device_id_type=MESH)

    pl.semaphore_wait(barrier, 15 + has_left.astype(jnp.int32) + has_right.astype(jnp.int32))

    for c in range(AHEAD):
        start_surfaces(c)

    def clear(i, carry):
        zero = jnp.zeros((NB, NB), BF)
        gpad[i] = zero
        gpad[2 * PER + i] = zero
        return carry

    lax.fori_loop(0, PER, clear, 0)

    @pl.when(jnp.logical_not(has_lower))
    def _():
        def fill(i, carry):
            win[i] = jnp.zeros((NB, NB), BF)
            return carry

        lax.fori_loop(0, PER, fill, 0)

    @pl.when(jnp.logical_not(has_left))
    def _():
        def fill(i, carry):
            left_in[i] = jnp.zeros((HALF, HALF), BF)
            return carry

        lax.fori_loop(0, PER, fill, 0)

    @pl.when(jnp.logical_not(has_right))
    def _():
        def fill(i, carry):
            right_in[i] = jnp.zeros((HALF, HALF), BF)
            return carry

        lax.fori_loop(0, PER, fill, 0)

    def clear_acc(w, carry):
        acc[w] = jnp.zeros((NB, NB), F32)
        return carry

    lax.fori_loop(0, W, clear_acc, 0)

    for c in range(STEPS):
        g_copy(c).wait()

    def correlate(s_base, g_base):
        def one(t, carry):
            rows = pl.ds(pl.multiple_of(t * ROWS, ROWS), ROWS)
            held = [win[s_base + i, rows, :] for i in range(CH)]
            for w in range(W):
                at = g_base + shifts[w]
                terms = [held[i] * gpad[at + i, rows, :] for i in range(CH)]
                acc[w, rows, :] += tree(terms).astype(F32)
            return carry

        lax.fori_loop(0, NB // ROWS, one, 0)

    a = grad[...]
    lc = left_cpl[...]
    rc = right_cpl[...]

    def step(c, carry):
        e0 = c * CH
        for i in range(CH):
            first[pl.ds(i * NB, NB), :] = nn(a, gpad[PER + e0 + i]).astype(BF)

        @pl.when(has_left)
        def _():
            left_copy(c).wait_recv()

        @pl.when(has_right)
        def _():
            right_copy(c).wait_recv()

        lp = [nn(lc, left_in[e0 + i]).astype(BF) for i in range(CH)]
        rp = [nn(rc, right_in[e0 + i]).astype(BF) for i in range(CH)]
        for i in range(CH):
            total = nt(first[pl.ds(i * NB, NB), :], a) + nt(lp[i], lc) + nt(rp[i], rc)
            win[PER + e0 + i] = total.astype(BF)

        aside = jnp.logical_and(me == crossing, relayed(c))

        @pl.when(jnp.logical_and(has_upper, jnp.logical_not(aside)))
        def _():
            up_copy(c).start()

        @pl.when(aside)
        def _():
            aside_copy(c).start()

        @pl.when(has_right)
        def _():
            left_copy(c).wait_send()

        @pl.when(has_left)
        def _():
            right_copy(c).wait_send()

        @pl.when(c + AHEAD < STEPS)
        def _():
            start_surfaces(c + AHEAD)

        correlate(PER + e0, PER + e0)

        @pl.when(c >= LAG)
        def _():
            @pl.when(has_lower)
            def _():
                up_copy(c - LAG).wait_recv()

            correlate(e0 - LAG * CH, e0 - LAG * CH)

        before = jnp.maximum(c - 1, 0)

        @pl.when(jnp.logical_and(c > 0, jnp.logical_and(relayed(before), me == relay_of(before))))
        def _():
            aside_copy(before).wait_recv()
            relay_copy(before).start()

        return carry

    lax.fori_loop(0, STEPS, step, 0)

    def core_copy(j):
        return pltpu.make_async_remote_copy(
            src_ref=part.at[j], dst_ref=from_core.at[j], send_sem=c1s.at[j], recv_sem=c1r.at[j],
            device_id=partner, device_id_type=MESH)

    last = PER - CH
    for c in range(STEPS - LAG, STEPS):
        @pl.when(has_lower)
        def _():
            up_copy(c).wait_recv()

        if c < STEPS - 1:
            correlate(c * CH, c * CH)

    def finish(w, store):
        at = last + shifts[w]

        def one(t, carry):
            rows = pl.ds(pl.multiple_of(t * ROWS, ROWS), ROWS)
            terms = [win[last + i, rows, :] * gpad[at + i, rows, :] for i in range(CH)]
            store(rows, (acc[w, rows, :] + tree(terms).astype(F32)) * scale)
            return carry

        lax.fori_loop(0, NB // ROWS, one, 0)

    def theirs(k, carry):
        j = lax.rem(chip + k, CHIPS)

        def store(rows, value):
            part[j, rows, :] = value.astype(BF)

        finish(2 * j + 1 - core, store)
        core_copy(j).start()
        return carry

    lax.fori_loop(1, CHIPS + 1, theirs, 0)

    def ours(k, carry):
        j = lax.rem(chip + k, CHIPS)
        w = 2 * j + core

        def store(rows, value):
            acc[w, rows, :] = value

        finish(w, store)
        return carry

    lax.fori_loop(1, CHIPS + 1, ours, 0)

    def chip_copy(k):
        return pltpu.make_async_remote_copy(
            src_ref=sums.at[k - 1], dst_ref=from_chip.at[k - 1], send_sem=c2s.at[k - 1], recv_sem=c2r.at[k - 1],
            device_id={"energy": 2 * lax.rem(chip + k, CHIPS) + core, "layer": layer}, device_id_type=MESH)

    def join(k, carry):
        j = lax.rem(chip + k, CHIPS)
        w = 2 * j + core
        core_copy(j).wait_recv()

        def one(t, c2):
            rows = pl.ds(pl.multiple_of(t * ROWS, ROWS), ROWS)
            sums[k - 1, rows, :] = (acc[w, rows, :] + from_core[j, rows, :].astype(F32)).astype(BF)
            return c2

        lax.fori_loop(0, NB // ROWS, one, 0)
        chip_copy(k).start()
        return carry

    lax.fori_loop(1, CHIPS, join, 0)
    core_copy(chip).wait_recv()
    for k in range(1, CHIPS):
        chip_copy(k).wait_recv()

    def total_rows(t, carry):
        rows = pl.ds(pl.multiple_of(t * ROWS, ROWS), ROWS)
        value = acc[me, rows, :] + from_core[chip, rows, :].astype(F32)
        for k in range(CHIPS - 1):
            value = value + from_chip[k, rows, :].astype(F32)
        self_out[rows, :] = value
        return carry

    lax.fori_loop(0, NB // ROWS, total_rows, 0)

    on_diag = lax.broadcasted_iota(jnp.int32, (NB, NB), 0) == lax.broadcasted_iota(jnp.int32, (NB, NB), 1)
    matrix = stiff[...] + COUPLING * self_out[...]
    matrix = matrix + jnp.where(on_diag, omega[me], 0.0)
    diag = jnp.where(on_diag, matrix, 0.0)
    inv_row = 1.0 / jnp.sum(diag, axis=0, keepdims=True)
    inv_col = 1.0 / jnp.sum(diag, axis=1, keepdims=True)
    approx = jnp.where(on_diag, 2.0 * inv_col, 0.0) - inv_col * (matrix * inv_row)
    for _ in range(NEWTON - 1):
        product = nn(matrix, approx, precision=lax.Precision.HIGHEST)
        approx = 2.0 * approx - nn(approx, product, precision=lax.Precision.HIGHEST)
    green_out[...] = approx
    rounded[me] = approx.astype(BF)

    def gather_copy(k):
        return pltpu.make_async_remote_copy(
            src_ref=rounded.at[me], dst_ref=rounded.at[me], send_sem=gs.at[k - 1], recv_sem=gr.at[k - 1],
            device_id={"energy": 2 * lax.rem(chip + k, CHIPS) + core, "layer": layer}, device_id_type=MESH)

    def gather_arrival(k):
        w = 2 * lax.rem(chip + CHIPS - k, CHIPS) + core
        return pltpu.make_async_remote_copy(
            src_ref=rounded.at[w], dst_ref=rounded.at[w], send_sem=gs.at[k - 1], recv_sem=gr.at[k - 1],
            device_id={"energy": w, "layer": layer}, device_id_type=MESH)

    def pass_on(k, whose):
        w = 2 * lax.rem(chip + CHIPS - k, CHIPS) + whose
        return pltpu.make_async_remote_copy(
            src_ref=rounded.at[w], dst_ref=rounded.at[w], send_sem=fs.at[k], recv_sem=fr.at[k],
            device_id=partner, device_id_type=MESH)

    pass_on(0, core).start()
    for k in range(1, CHIPS):
        gather_copy(k).start()

    group = 4
    for g in range(W // group):
        ws = []
        for k in (2 * g, 2 * g + 1):
            if k > 0:
                gather_arrival(k).wait_recv()
                pass_on(k, core).start()
        for k in (2 * g, 2 * g + 1):
            pass_on(k, 1 - core).wait_recv()
            owner = 2 * lax.rem(chip + CHIPS - k, CHIPS)
            ws += [owner, owner + 1]
        final = g == W // group - 1

        def mix_rows(t, carry):
            rows = pl.ds(pl.multiple_of(t * ROWS, ROWS), ROWS)
            held = [rounded[w, rows, :] for w in ws]
            ats = [PER - shifts[w] for w in ws]
            for e in range(PER):
                terms = [held[i] * win[ats[i] + e, rows, :] for i in range(group)]
                value = tree(terms).astype(F32)
                if g > 0:
                    value = mix[e, rows, :] + value
                if final:
                    tile[pl.ds(e * ROWS, ROWS), :] = value.astype(BF)
                else:
                    mix[e, rows, :] = value
            if final:
                out = nt(tile[...], a).astype(BF)
                for e in range(PER):
                    turned[e, rows, :] = out[e * ROWS:(e + 1) * ROWS]
                turn_copy(t).start()
            return carry

        def turn_copy(t):
            rows = pl.ds(pl.multiple_of(t * ROWS, ROWS), ROWS)
            return pltpu.make_async_copy(turned.at[:, rows, :], turned_out.at[:, rows, :], ts.at[t])

        lax.fori_loop(0, NB // ROWS, mix_rows, 0)

    for t in range(NB // ROWS):
        turn_copy(t).wait()
    for c in range(STEPS):
        @pl.when(has_upper)
        def _():
            up_copy(c).wait_send()

        if c % 4 < 3:
            @pl.when(me == relay_of(c))
            def _():
                relay_copy(c).wait_send()
    for j in range(CHIPS):
        core_copy(j).wait_send()
        pass_on(j, core).wait_send()
    for k in range(1, CHIPS):
        chip_copy(k).wait_send()
        gather_copy(k).wait_send()


def last_kernel(grad, turned, self_in, green_in, out, self_out, green_out):
    a = grad[...]
    for i in range(LAST):
        out[i] = nn(a, turned[i]).astype(BF)
    self_out[...] = self_in[...]
    green_out[...] = green_in[...]


def body(green, gradient, left_coupling, right_coupling, dynamical, omega_sq, shifts):
    scale = 1.0 / math.sqrt(PER * lax.axis_size("energy"))
    vmem = pl.BlockSpec(memory_space=pltpu.VMEM)
    smem = pl.BlockSpec(memory_space=pltpu.SMEM)
    hbm = pl.BlockSpec(memory_space=pl.ANY)
    dma = pltpu.SemaphoreType.DMA
    own_self, own_green, turned = pl.pallas_call(
        functools.partial(scatter_kernel, scale),
        out_shape=[
            jax.ShapeDtypeStruct((NB, NB), F32),
            jax.ShapeDtypeStruct((NB, NB), F32),
            jax.ShapeDtypeStruct((PER, NB, NB), BF),
        ],
        in_specs=[smem, smem, hbm, vmem, vmem, vmem, vmem],
        out_specs=[vmem, vmem, hbm],
        scratch_shapes=[
            pltpu.VMEM((3 * PER, NB, NB), BF),
            pltpu.VMEM((2 * PER, NB, NB), BF),
            pltpu.VMEM((PER, HALF, HALF), BF),
            pltpu.VMEM((PER, HALF, HALF), BF),
            pltpu.VMEM((CH * NB, NB), BF),
            pltpu.VMEM((W, NB, NB), F32),
            pltpu.VMEM((CHIPS, NB, NB), BF),
            pltpu.VMEM((CHIPS - 1, NB, NB), BF),
            pltpu.VMEM((CHIPS, NB, NB), BF),
            pltpu.VMEM((CHIPS - 1, NB, NB), BF),
            pltpu.VMEM((W, NB, NB), BF),
            pltpu.VMEM((PER, NB, NB), F32),
            pltpu.VMEM((PER * ROWS, NB), BF),
            pltpu.VMEM((PER, NB, NB), BF),
            pltpu.VMEM((PER // 4, NB, NB), BF),
            dma((STEPS,)),
            dma((STEPS,)), dma((STEPS,)), dma((STEPS,)), dma((STEPS,)), dma((STEPS,)), dma((STEPS,)),
            dma((CHIPS,)), dma((CHIPS,)), dma((CHIPS - 1,)), dma((CHIPS - 1,)),
            dma((CHIPS - 1,)), dma((CHIPS - 1,)), dma((CHIPS,)), dma((CHIPS,)),
            dma((NB // ROWS,)), dma((STEPS // 4,)), dma((STEPS // 4,)),
        ],
        compiler_params=pltpu.CompilerParams(
            collective_id=0, has_side_effects=True, vmem_limit_bytes=58 << 20),
        name="scatter",
    )(shifts, omega_sq, green[:, 0], gradient[0], left_coupling[0], right_coupling[0], dynamical[0])
    steps = PER // LAST
    block = pl.BlockSpec((LAST, NB, NB), lambda i: (i, 0, 0))
    whole = pl.BlockSpec((NB, NB), lambda i: (0, 0))
    piece = pl.BlockSpec((NB // steps, NB), lambda i: (i, 0))
    electron, own_self, own_green = pl.pallas_call(
        last_kernel,
        grid=(steps,),
        in_specs=[whole, block, piece, piece],
        out_specs=[block, piece, piece],
        out_shape=[
            jax.ShapeDtypeStruct((PER, NB, NB), BF),
            jax.ShapeDtypeStruct((NB, NB), F32),
            jax.ShapeDtypeStruct((NB, NB), F32),
        ],
        name="last",
    )(gradient[0], turned, own_self, own_green)
    return own_self[None, None], own_green[None, None], electron[:, None]


def solution(mesh):
    return jax.shard_map(
        body,
        mesh=mesh,
        in_specs=(
            P("energy", "layer", None, None),
            P("layer", None, None),
            P("layer", None, None),
            P("layer", None, None),
            P("layer", None, None),
            P(),
            P(),
        ),
        out_specs=(
            P("energy", "layer", None, None),
            P("energy", "layer", None, None),
            P("energy", "layer", None, None),
        ),
        check_vma=False,
    )
```

```python
import functools
import math

import jax
import jax.numpy as jnp
from jax import lax
from jax.experimental import pallas as pl
from jax.experimental.pallas import tpu as pltpu
from jax.sharding import PartitionSpec as P

NEWTON = 3
COUPLING = 0.01
MESH = pl.DeviceIdType.MESH
BF = jnp.bfloat16
F32 = jnp.float32

PER = 32
NB = 256
HALF = 128
CH = 2
STEPS = PER // CH
AHEAD = 4
LAG = 4
W = 16
CHIPS = 8
LAST = 16
SPLIT = 16
QUAD = 4
DOWN = SPLIT // 4
ROWS = 32


def nn(a, b, **kw):
    return lax.dot_general(a, b, (((1,), (0,)), ((), ())), preferred_element_type=F32, **kw)


def nt(a, b, **kw):
    return lax.dot_general(a, b, (((1,), (1,)), ((), ())), preferred_element_type=F32, **kw)


def tree(terms):
    while len(terms) > 1:
        terms = [terms[i] + terms[i + 1] if i + 1 < len(terms) else terms[i] for i in range(0, len(terms), 2)]
    return terms[0]


def scatter_kernel(
    scale, shifts, omega, green, grad, left_cpl, right_cpl, stiff,
    self_out, green_out, turned_out,
    gown, glow, win, left_in, right_in, first, acc, part, sums, from_core, from_chip, rounded, mix, tile, turned, held_over, held_green,
    g_sem, ls, lr, rs, rr, us, ur, c1s, c1r, c2s, c2r, gs, gr, fs, fr, ts, hs, hr,
    low_sem, ds, dr, ks, kr,
):
    me = lax.axis_index("energy")
    layer = lax.axis_index("layer")
    core = lax.rem(me, 2)
    chip = me // 2
    has_lower, has_upper = me > 0, me < 15
    has_left, has_right = layer > 0, layer < 7
    partner = {"energy": me + 1 - 2 * core, "layer": layer}

    def g_copy(c):
        return pltpu.make_async_copy(
            green.at[pl.ds(c * CH, CH)], gown.at[pl.ds(c * CH, CH)], g_sem.at[c])

    def left_copy(c):
        return pltpu.make_async_remote_copy(
            src_ref=green.at[pl.ds(c * CH, CH), pl.ds(HALF, HALF), pl.ds(HALF, HALF)],
            dst_ref=left_in.at[pl.ds(c * CH, CH)], send_sem=ls.at[c], recv_sem=lr.at[c],
            device_id={"energy": me, "layer": lax.rem(layer + 1, 8)}, device_id_type=MESH)

    def right_copy(c):
        return pltpu.make_async_remote_copy(
            src_ref=green.at[pl.ds(c * CH, CH), pl.ds(0, HALF), pl.ds(0, HALF)],
            dst_ref=right_in.at[pl.ds(c * CH, CH)], send_sem=rs.at[c], recv_sem=rr.at[c],
            device_id={"energy": me, "layer": lax.rem(layer + 7, 8)}, device_id_type=MESH)

    def up_copy(c):
        return pltpu.make_async_remote_copy(
            src_ref=win.at[pl.ds(PER + c * CH, CH)], dst_ref=win.at[pl.ds(c * CH, CH)],
            send_sem=us.at[c], recv_sem=ur.at[c],
            device_id={"energy": lax.rem(me + 1, 16), "layer": layer}, device_id_type=MESH)

    crossing = 7

    def relay_of(c):
        return lax.rem(4 * lax.rem(c, 4), 6)

    def relayed(c):
        return lax.rem(c, 4) < 3

    def aside_copy(c):
        return pltpu.make_async_remote_copy(
            src_ref=win.at[pl.ds(PER + c * CH, CH)], dst_ref=held_over.at[pl.ds(c // 4 * CH, CH)],
            send_sem=us.at[c], recv_sem=hr.at[c // 4],
            device_id={"energy": relay_of(c), "layer": layer}, device_id_type=MESH)

    def relay_copy(c):
        return pltpu.make_async_remote_copy(
            src_ref=held_over.at[pl.ds(c // 4 * CH, CH)], dst_ref=win.at[pl.ds(c * CH, CH)],
            send_sem=hs.at[c // 4], recv_sem=ur.at[c],
            device_id={"energy": crossing + 1, "layer": layer}, device_id_type=MESH)

    def down_copy(p):
        return pltpu.make_async_remote_copy(
            src_ref=green.at[pl.ds(p * DOWN, DOWN)], dst_ref=gown.at[pl.ds(PER + p * DOWN, DOWN)],
            send_sem=ds.at[p], recv_sem=dr.at[p],
            device_id={"energy": lax.rem(me + 15, 16), "layer": layer}, device_id_type=MESH)

    def down_aside(p):
        return pltpu.make_async_remote_copy(
            src_ref=green.at[pl.ds(p * DOWN, DOWN)], dst_ref=held_green, send_sem=ds.at[p], recv_sem=kr,
            device_id={"energy": 14 - 2 * p, "layer": layer}, device_id_type=MESH)

    def down_relay(p):
        return pltpu.make_async_remote_copy(
            src_ref=held_green, dst_ref=gown.at[pl.ds(PER + p * DOWN, DOWN)], send_sem=ks, recv_sem=dr.at[p],
            device_id={"energy": crossing, "layer": layer}, device_id_type=MESH)

    low_copy = pltpu.make_async_copy(green.at[pl.ds(SPLIT, PER - SPLIT)], glow.at[pl.ds(PER, PER - SPLIT)], low_sem)

    def start_surfaces(step):
        c = STEPS - 1 - step
        @pl.when(has_right)
        def _():
            left_copy(c).start()

        @pl.when(has_left)
        def _():
            right_copy(c).start()

    for c in reversed(range(STEPS)):
        g_copy(c).start()
    low_copy.start()

    barrier = pltpu.get_barrier_semaphore()
    for k in range(1, 16):
        pl.semaphore_signal(
            barrier, inc=1, device_id={"energy": lax.rem(me + k, 16), "layer": layer}, device_id_type=MESH)

    @pl.when(has_right)
    def _():
        pl.semaphore_signal(barrier, inc=1, device_id={"energy": me, "layer": layer + 1}, device_id_type=MESH)

    @pl.when(has_left)
    def _():
        pl.semaphore_signal(barrier, inc=1, device_id={"energy": me, "layer": layer - 1}, device_id_type=MESH)

    pl.semaphore_wait(barrier, 15 + has_left.astype(jnp.int32) + has_right.astype(jnp.int32))

    for c in range(AHEAD):
        start_surfaces(c)

    for p in range(4):
        split_path = me == crossing + 1 if p < 3 else me < 0

        @pl.when(jnp.logical_and(has_lower, jnp.logical_not(split_path)))
        def _():
            down_copy(p).start()

        @pl.when(split_path)
        def _():
            down_aside(p).start()

    def clear(i, carry):
        zero = jnp.zeros((NB, NB), BF)
        glow[i] = zero
        return carry

    lax.fori_loop(0, PER, clear, 0)

    def clear_top(i, carry):
        gown[i] = jnp.zeros((NB, NB), BF)
        return carry

    lax.fori_loop(PER + SPLIT, 2 * PER, clear_top, 0)

    @pl.when(jnp.logical_not(has_upper))
    def _():
        lax.fori_loop(PER, PER + SPLIT, clear_top, 0)

    @pl.when(jnp.logical_not(has_lower))
    def _():
        def fill(i, carry):
            win[i] = jnp.zeros((NB, NB), BF)
            return carry

        lax.fori_loop(0, PER, fill, 0)

    @pl.when(jnp.logical_not(has_left))
    def _():
        def fill(i, carry):
            left_in[i] = jnp.zeros((HALF, HALF), BF)
            return carry

        lax.fori_loop(0, PER, fill, 0)

    @pl.when(jnp.logical_not(has_right))
    def _():
        def fill(i, carry):
            right_in[i] = jnp.zeros((HALF, HALF), BF)
            return carry

        lax.fori_loop(0, PER, fill, 0)

    def clear_acc(w, carry):
        acc[w] = jnp.zeros((NB, NB), F32)
        return carry

    lax.fori_loop(0, W, clear_acc, 0)

    for c in range(STEPS):
        g_copy(c).wait()
    low_copy.wait()

    def correlate(s_base, green_ref, g_base):
        def one(t, carry):
            rows = pl.ds(pl.multiple_of(t * ROWS, ROWS), ROWS)
            held = [win[s_base + i, rows, :] for i in range(QUAD)]
            for w in range(W):
                at = g_base + shifts[w]
                terms = [held[i] * green_ref[at + i, rows, :] for i in range(QUAD)]
                acc[w, rows, :] += tree(terms).astype(F32)
            return carry

        lax.fori_loop(0, NB // ROWS, one, 0)

    a = grad[...]
    lc = left_cpl[...]
    rc = right_cpl[...]

    def step(at_step, carry):
        c = STEPS - 1 - at_step
        e0 = c * CH
        for i in range(CH):
            first[pl.ds(i * NB, NB), :] = nn(a, gown[e0 + i]).astype(BF)

        @pl.when(has_left)
        def _():
            left_copy(c).wait_recv()

        @pl.when(has_right)
        def _():
            right_copy(c).wait_recv()

        lp = [nn(lc, left_in[e0 + i]).astype(BF) for i in range(CH)]
        rp = [nn(rc, right_in[e0 + i]).astype(BF) for i in range(CH)]
        for i in range(CH):
            total = nt(first[pl.ds(i * NB, NB), :], a) + nt(lp[i], lc) + nt(rp[i], rc)
            win[PER + e0 + i] = total.astype(BF)

        needed = c >= SPLIT // CH
        aside = jnp.logical_and(me == crossing, jnp.logical_and(needed, relayed(c)))
        later = jnp.logical_and(me == crossing, jnp.logical_not(needed))

        @pl.when(jnp.logical_and(has_upper, jnp.logical_not(jnp.logical_or(aside, later))))
        def _():
            up_copy(c).start()

        @pl.when(aside)
        def _():
            aside_copy(c).start()

        @pl.when(has_right)
        def _():
            left_copy(c).wait_send()

        @pl.when(has_left)
        def _():
            right_copy(c).wait_send()

        @pl.when(at_step + AHEAD < STEPS)
        def _():
            start_surfaces(at_step + AHEAD)

        low = c + LAG
        pair = jnp.logical_and(low < STEPS, jnp.logical_and(low >= SPLIT // CH, lax.rem(at_step - LAG + 2 * STEPS, 2) == 1))

        @pl.when(pair)
        def _():
            @pl.when(has_lower)
            def _():
                up_copy(low + 1).wait_recv()
                up_copy(low).wait_recv()

            correlate(low * CH, glow, low * CH - SPLIT)

        @pl.when(at_step == STEPS // 2)
        def _():
            @pl.when(has_upper)
            def _():
                for p in range(4):
                    down_copy(p).wait_recv()

        @pl.when(jnp.logical_and(at_step >= STEPS // 2, c > 0))
        def _():
            top = PER - QUAD - (at_step - STEPS // 2) * QUAD
            correlate(PER + top, gown, top)

        before = jnp.minimum(c + 1, STEPS - 1)

        @pl.when(jnp.logical_and(
            jnp.logical_and(at_step > 0, before >= SPLIT // CH), jnp.logical_and(relayed(before), me == relay_of(before))))
        def _():
            aside_copy(before).wait_recv()
            relay_copy(before).start()

        for p in range(3):
            @pl.when(jnp.logical_and(at_step == 2, me == 14 - 2 * p))
            def _():
                down_aside(p).wait_recv()
                down_relay(p).start()

        return carry

    lax.fori_loop(0, STEPS, step, 0)

    for c in reversed(range(SPLIT // CH)):
        @pl.when(me == crossing)
        def _():
            (aside_copy(c) if c % 4 < 3 else up_copy(c)).start()

    def core_copy(j):
        return pltpu.make_async_remote_copy(
            src_ref=part.at[j], dst_ref=from_core.at[j], send_sem=c1s.at[j], recv_sem=c1r.at[j],
            device_id=partner, device_id_type=MESH)

    def finish(w, store):
        at = shifts[w]

        def one(t, carry):
            rows = pl.ds(pl.multiple_of(t * ROWS, ROWS), ROWS)
            terms = [win[PER + i, rows, :] * gown[at + i, rows, :] for i in range(QUAD)]
            store(rows, (acc[w, rows, :] + tree(terms).astype(F32)) * scale)
            return carry

        lax.fori_loop(0, NB // ROWS, one, 0)

    def theirs(k, carry):
        j = lax.rem(chip + k, CHIPS)

        def store(rows, value):
            part[j, rows, :] = value.astype(BF)

        finish(2 * j + 1 - core, store)
        core_copy(j).start()
        return carry

    lax.fori_loop(1, CHIPS + 1, theirs, 0)

    def ours(k, carry):
        j = lax.rem(chip + k, CHIPS)
        w = 2 * j + core

        def store(rows, value):
            acc[w, rows, :] = value

        finish(w, store)
        return carry

    lax.fori_loop(1, CHIPS + 1, ours, 0)

    def chip_copy(k):
        return pltpu.make_async_remote_copy(
            src_ref=sums.at[k - 1], dst_ref=from_chip.at[k - 1], send_sem=c2s.at[k - 1], recv_sem=c2r.at[k - 1],
            device_id={"energy": 2 * lax.rem(chip + k, CHIPS) + core, "layer": layer}, device_id_type=MESH)

    def join(k, carry):
        j = lax.rem(chip + k, CHIPS)
        w = 2 * j + core
        core_copy(j).wait_recv()

        def one(t, c2):
            rows = pl.ds(pl.multiple_of(t * ROWS, ROWS), ROWS)
            sums[k - 1, rows, :] = (acc[w, rows, :] + from_core[j, rows, :].astype(F32)).astype(BF)
            return c2

        lax.fori_loop(0, NB // ROWS, one, 0)
        chip_copy(k).start()
        return carry

    lax.fori_loop(1, CHIPS, join, 0)

    for c in reversed(range(SPLIT // CH)):
        if c % 4 < 3:
            @pl.when(me == relay_of(c))
            def _():
                aside_copy(c).wait_recv()
                relay_copy(c).start()

    core_copy(chip).wait_recv()
    for k in range(1, CHIPS):
        chip_copy(k).wait_recv()

    def total_rows(t, carry):
        rows = pl.ds(pl.multiple_of(t * ROWS, ROWS), ROWS)
        value = acc[me, rows, :] + from_core[chip, rows, :].astype(F32)
        for k in range(CHIPS - 1):
            value = value + from_chip[k, rows, :].astype(F32)
        self_out[rows, :] = value
        return carry

    lax.fori_loop(0, NB // ROWS, total_rows, 0)

    on_diag = lax.broadcasted_iota(jnp.int32, (NB, NB), 0) == lax.broadcasted_iota(jnp.int32, (NB, NB), 1)
    matrix = stiff[...] + COUPLING * self_out[...]
    matrix = matrix + jnp.where(on_diag, omega[me], 0.0)
    diag = jnp.where(on_diag, matrix, 0.0)
    inv_row = 1.0 / jnp.sum(diag, axis=0, keepdims=True)
    inv_col = 1.0 / jnp.sum(diag, axis=1, keepdims=True)
    approx = jnp.where(on_diag, 2.0 * inv_col, 0.0) - inv_col * (matrix * inv_row)
    for _ in range(NEWTON - 1):
        product = nn(matrix, approx, precision=lax.Precision.HIGHEST)
        approx = 2.0 * approx - nn(approx, product, precision=lax.Precision.HIGHEST)
    green_out[...] = approx
    rounded[me] = approx.astype(BF)

    def gather_copy(k):
        return pltpu.make_async_remote_copy(
            src_ref=rounded.at[me], dst_ref=rounded.at[me], send_sem=gs.at[k - 1], recv_sem=gr.at[k - 1],
            device_id={"energy": 2 * lax.rem(chip + k, CHIPS) + core, "layer": layer}, device_id_type=MESH)

    def gather_arrival(k):
        w = 2 * lax.rem(chip + CHIPS - k, CHIPS) + core
        return pltpu.make_async_remote_copy(
            src_ref=rounded.at[w], dst_ref=rounded.at[w], send_sem=gs.at[k - 1], recv_sem=gr.at[k - 1],
            device_id={"energy": w, "layer": layer}, device_id_type=MESH)

    def pass_on(k, whose):
        w = 2 * lax.rem(chip + CHIPS - k, CHIPS) + whose
        return pltpu.make_async_remote_copy(
            src_ref=rounded.at[w], dst_ref=rounded.at[w], send_sem=fs.at[k], recv_sem=fr.at[k],
            device_id=partner, device_id_type=MESH)

    pass_on(0, core).start()
    for k in range(1, CHIPS):
        gather_copy(k).start()

    for c in range(SPLIT // CH):
        @pl.when(has_lower)
        def _():
            up_copy(c).wait_recv()

    group = 4
    for g in range(W // group):
        ws = []
        for k in (2 * g, 2 * g + 1):
            if k > 0:
                gather_arrival(k).wait_recv()
                pass_on(k, core).start()
        for k in (2 * g, 2 * g + 1):
            pass_on(k, 1 - core).wait_recv()
            owner = 2 * lax.rem(chip + CHIPS - k, CHIPS)
            ws += [owner, owner + 1]
        final = g == W // group - 1

        def mix_rows(t, carry):
            rows = pl.ds(pl.multiple_of(t * ROWS, ROWS), ROWS)
            held = [rounded[w, rows, :] for w in ws]
            ats = [PER - shifts[w] for w in ws]
            for e in range(PER):
                terms = [held[i] * win[ats[i] + e, rows, :] for i in range(group)]
                value = tree(terms).astype(F32)
                if g > 0:
                    value = mix[e, rows, :] + value
                if final:
                    tile[pl.ds(e * ROWS, ROWS), :] = value.astype(BF)
                else:
                    mix[e, rows, :] = value
            if final:
                out = nt(tile[...], a).astype(BF)
                for e in range(PER):
                    turned[e, rows, :] = out[e * ROWS:(e + 1) * ROWS]
                turn_copy(t).start()
            return carry

        def turn_copy(t):
            rows = pl.ds(pl.multiple_of(t * ROWS, ROWS), ROWS)
            return pltpu.make_async_copy(turned.at[:, rows, :], turned_out.at[:, rows, :], ts.at[t])

        lax.fori_loop(0, NB // ROWS, mix_rows, 0)

    for t in range(NB // ROWS):
        turn_copy(t).wait()
    for c in range(STEPS):
        @pl.when(has_upper)
        def _():
            up_copy(c).wait_send()

        if c % 4 < 3:
            @pl.when(me == relay_of(c))
            def _():
                relay_copy(c).wait_send()
    for p in range(4):
        @pl.when(has_lower)
        def _():
            down_copy(p).wait_send()

        if p < 3:
            @pl.when(me == 14 - 2 * p)
            def _():
                down_relay(p).wait_send()
    for j in range(CHIPS):
        core_copy(j).wait_send()
        pass_on(j, core).wait_send()
    for k in range(1, CHIPS):
        chip_copy(k).wait_send()
        gather_copy(k).wait_send()


def last_kernel(grad, turned, self_in, green_in, out, self_out, green_out):
    a = grad[...]
    for i in range(LAST):
        out[i] = nn(a, turned[i]).astype(BF)
    self_out[...] = self_in[...]
    green_out[...] = green_in[...]


def body(green, gradient, left_coupling, right_coupling, dynamical, omega_sq, shifts):
    scale = 1.0 / math.sqrt(PER * lax.axis_size("energy"))
    vmem = pl.BlockSpec(memory_space=pltpu.VMEM)
    smem = pl.BlockSpec(memory_space=pltpu.SMEM)
    hbm = pl.BlockSpec(memory_space=pl.ANY)
    dma = pltpu.SemaphoreType.DMA
    own_self, own_green, turned = pl.pallas_call(
        functools.partial(scatter_kernel, scale),
        out_shape=[
            jax.ShapeDtypeStruct((NB, NB), F32),
            jax.ShapeDtypeStruct((NB, NB), F32),
            jax.ShapeDtypeStruct((PER, NB, NB), BF),
        ],
        in_specs=[smem, smem, hbm, vmem, vmem, vmem, vmem],
        out_specs=[vmem, vmem, hbm],
        scratch_shapes=[
            pltpu.VMEM((2 * PER, NB, NB), BF),
            pltpu.VMEM((2 * PER - SPLIT, NB, NB), BF),
            pltpu.VMEM((2 * PER, NB, NB), BF),
            pltpu.VMEM((PER, HALF, HALF), BF),
            pltpu.VMEM((PER, HALF, HALF), BF),
            pltpu.VMEM((CH * NB, NB), BF),
            pltpu.VMEM((W, NB, NB), F32),
            pltpu.VMEM((CHIPS, NB, NB), BF),
            pltpu.VMEM((CHIPS - 1, NB, NB), BF),
            pltpu.VMEM((CHIPS, NB, NB), BF),
            pltpu.VMEM((CHIPS - 1, NB, NB), BF),
            pltpu.VMEM((W, NB, NB), BF),
            pltpu.VMEM((PER, NB, NB), F32),
            pltpu.VMEM((PER * ROWS, NB), BF),
            pltpu.VMEM((PER, NB, NB), BF),
            pltpu.VMEM((PER // 4, NB, NB), BF),
            pltpu.VMEM((DOWN, NB, NB), BF),
            dma((STEPS,)),
            dma((STEPS,)), dma((STEPS,)), dma((STEPS,)), dma((STEPS,)), dma((STEPS,)), dma((STEPS,)),
            dma((CHIPS,)), dma((CHIPS,)), dma((CHIPS - 1,)), dma((CHIPS - 1,)),
            dma((CHIPS - 1,)), dma((CHIPS - 1,)), dma((CHIPS,)), dma((CHIPS,)),
            dma((NB // ROWS,)), dma((STEPS // 4,)), dma((STEPS // 4,)),
            dma, dma((4,)), dma((4,)), dma, dma,
        ],
        compiler_params=pltpu.CompilerParams(
            collective_id=0, has_side_effects=True, vmem_limit_bytes=58 << 20),
        name="scatter",
    )(shifts, omega_sq, green[:, 0], gradient[0], left_coupling[0], right_coupling[0], dynamical[0])
    steps = PER // LAST
    block = pl.BlockSpec((LAST, NB, NB), lambda i: (i, 0, 0))
    whole = pl.BlockSpec((NB, NB), lambda i: (0, 0))
    piece = pl.BlockSpec((NB // steps, NB), lambda i: (i, 0))
    electron, own_self, own_green = pl.pallas_call(
        last_kernel,
        grid=(steps,),
        in_specs=[whole, block, piece, piece],
        out_specs=[block, piece, piece],
        out_shape=[
            jax.ShapeDtypeStruct((PER, NB, NB), BF),
            jax.ShapeDtypeStruct((NB, NB), F32),
            jax.ShapeDtypeStruct((NB, NB), F32),
        ],
        name="last",
    )(gradient[0], turned, own_self, own_green)
    return own_self[None, None], own_green[None, None], electron[:, None]


def solution(mesh):
    return jax.shard_map(
        body,
        mesh=mesh,
        in_specs=(
            P("energy", "layer", None, None),
            P("layer", None, None),
            P("layer", None, None),
            P("layer", None, None),
            P("layer", None, None),
            P(),
            P(),
        ),
        out_specs=(
            P("energy", "layer", None, None),
            P("energy", "layer", None, None),
            P("energy", "layer", None, None),
        ),
        check_vma=False,
    )
```

```python
import functools
import math

import jax
import jax.numpy as jnp
from jax import lax
from jax.experimental import pallas as pl
from jax.experimental.pallas import tpu as pltpu
from jax.sharding import PartitionSpec as P

NEWTON = 3
COUPLING = 0.01
MESH = pl.DeviceIdType.MESH
BF = jnp.bfloat16
F32 = jnp.float32

PER = 32
NB = 256
HALF = 128
CH = 2
STEPS = PER // CH
AHEAD = 4
LAG = 4
W = 16
CHIPS = 8
PLACES = ((0, 0), (1, 0), (0, 1), (0, 3), (1, 1), (1, 3), (0, 2), (1, 2))
STAGES = [[1, 2, 3], [4, 5, 6, 7]]
LAST = 16
SPLIT = 16
QUAD = 4
DOWN = SPLIT // 4
ROWS = 32


def nn(a, b, **kw):
    return lax.dot_general(a, b, (((1,), (0,)), ((), ())), preferred_element_type=F32, **kw)


def nt(a, b, **kw):
    return lax.dot_general(a, b, (((1,), (1,)), ((), ())), preferred_element_type=F32, **kw)


def halves(a):
    high = a.astype(BF)
    return high, (a - high.astype(F32)).astype(BF)


def nn_split(a, b):
    return nn(a[0], b[0]) + (nn(a[0], b[1]) + nn(a[1], b[0]))


def tree(terms):
    while len(terms) > 1:
        terms = [terms[i] + terms[i + 1] if i + 1 < len(terms) else terms[i] for i in range(0, len(terms), 2)]
    return terms[0]


def scatter_kernel(
    scale, shifts, omega, green, grad, left_cpl, right_cpl, stiff,
    self_out, green_out, mixture_out,
    gown, glow, win, left_in, right_in, first, acc, part, sums, from_core, from_chip, rounded, mix, mixture, held_over, held_green,
    g_sem, ls, lr, rs, rr, us, ur, c1s, c1r, c2s, c2r, gs, gr, fs, fr, ts, hs, hr,
    low_sem, ds, dr, ks, kr,
):
    me = lax.axis_index("energy")
    layer = lax.axis_index("layer")
    core = lax.rem(me, 2)
    chip = me // 2
    has_lower, has_upper = me > 0, me < 15
    has_left, has_right = layer > 0, layer < 7
    partner = {"energy": me + 1 - 2 * core, "layer": layer}

    def g_copy(c):
        return pltpu.make_async_copy(
            green.at[pl.ds(c * CH, CH)], gown.at[pl.ds(c * CH, CH)], g_sem.at[c])

    def left_copy(c):
        return pltpu.make_async_remote_copy(
            src_ref=green.at[pl.ds(c * CH, CH), pl.ds(HALF, HALF), pl.ds(HALF, HALF)],
            dst_ref=left_in.at[pl.ds(c * CH, CH)], send_sem=ls.at[c], recv_sem=lr.at[c],
            device_id={"energy": me, "layer": lax.rem(layer + 1, 8)}, device_id_type=MESH)

    def right_copy(c):
        return pltpu.make_async_remote_copy(
            src_ref=green.at[pl.ds(c * CH, CH), pl.ds(0, HALF), pl.ds(0, HALF)],
            dst_ref=right_in.at[pl.ds(c * CH, CH)], send_sem=rs.at[c], recv_sem=rr.at[c],
            device_id={"energy": me, "layer": lax.rem(layer + 7, 8)}, device_id_type=MESH)

    def up_copy(c):
        return pltpu.make_async_remote_copy(
            src_ref=win.at[pl.ds(PER + c * CH, CH)], dst_ref=win.at[pl.ds(c * CH, CH)],
            send_sem=us.at[c], recv_sem=ur.at[c],
            device_id={"energy": lax.rem(me + 1, 16), "layer": layer}, device_id_type=MESH)

    crossing = 7

    def relay_of(c):
        return lax.rem(4 * lax.rem(c, 4), 6)

    def relayed(c):
        return lax.rem(c, 4) < 3

    def aside_copy(c):
        return pltpu.make_async_remote_copy(
            src_ref=win.at[pl.ds(PER + c * CH, CH)], dst_ref=held_over.at[pl.ds(c // 4 * CH, CH)],
            send_sem=us.at[c], recv_sem=hr.at[c // 4],
            device_id={"energy": relay_of(c), "layer": layer}, device_id_type=MESH)

    def relay_copy(c):
        return pltpu.make_async_remote_copy(
            src_ref=held_over.at[pl.ds(c // 4 * CH, CH)], dst_ref=win.at[pl.ds(c * CH, CH)],
            send_sem=hs.at[c // 4], recv_sem=ur.at[c],
            device_id={"energy": crossing + 1, "layer": layer}, device_id_type=MESH)

    def down_copy(p):
        return pltpu.make_async_remote_copy(
            src_ref=green.at[pl.ds(p * DOWN, DOWN)], dst_ref=gown.at[pl.ds(PER + p * DOWN, DOWN)],
            send_sem=ds.at[p], recv_sem=dr.at[p],
            device_id={"energy": lax.rem(me + 15, 16), "layer": layer}, device_id_type=MESH)

    def down_aside(p):
        return pltpu.make_async_remote_copy(
            src_ref=green.at[pl.ds(p * DOWN, DOWN)], dst_ref=held_green, send_sem=ds.at[p], recv_sem=kr,
            device_id={"energy": 14 - 2 * p, "layer": layer}, device_id_type=MESH)

    def down_relay(p):
        return pltpu.make_async_remote_copy(
            src_ref=held_green, dst_ref=gown.at[pl.ds(PER + p * DOWN, DOWN)], send_sem=ks, recv_sem=dr.at[p],
            device_id={"energy": crossing, "layer": layer}, device_id_type=MESH)

    low_copy = pltpu.make_async_copy(green.at[pl.ds(SPLIT, PER - SPLIT)], glow.at[pl.ds(PER, PER - SPLIT)], low_sem)

    def start_surfaces(step):
        c = STEPS - 1 - step
        @pl.when(has_right)
        def _():
            left_copy(c).start()

        @pl.when(has_left)
        def _():
            right_copy(c).start()

    for c in reversed(range(STEPS)):
        g_copy(c).start()
    low_copy.start()

    barrier = pltpu.get_barrier_semaphore()
    for k in range(1, 16):
        pl.semaphore_signal(
            barrier, inc=1, device_id={"energy": lax.rem(me + k, 16), "layer": layer}, device_id_type=MESH)

    @pl.when(has_right)
    def _():
        pl.semaphore_signal(barrier, inc=1, device_id={"energy": me, "layer": layer + 1}, device_id_type=MESH)

    @pl.when(has_left)
    def _():
        pl.semaphore_signal(barrier, inc=1, device_id={"energy": me, "layer": layer - 1}, device_id_type=MESH)

    pl.semaphore_wait(barrier, 15 + has_left.astype(jnp.int32) + has_right.astype(jnp.int32))

    for c in range(AHEAD):
        start_surfaces(c)

    for p in range(4):
        split_path = me == crossing + 1 if p < 3 else me < 0

        @pl.when(jnp.logical_and(has_lower, jnp.logical_not(split_path)))
        def _():
            down_copy(p).start()

        @pl.when(split_path)
        def _():
            down_aside(p).start()

    def clear(i, carry):
        zero = jnp.zeros((NB, NB), BF)
        glow[i] = zero
        return carry

    lax.fori_loop(0, PER, clear, 0)

    def clear_top(i, carry):
        gown[i] = jnp.zeros((NB, NB), BF)
        return carry

    lax.fori_loop(PER + SPLIT, 2 * PER, clear_top, 0)

    @pl.when(jnp.logical_not(has_upper))
    def _():
        lax.fori_loop(PER, PER + SPLIT, clear_top, 0)

    @pl.when(jnp.logical_not(has_lower))
    def _():
        def fill(i, carry):
            win[i] = jnp.zeros((NB, NB), BF)
            return carry

        lax.fori_loop(0, PER, fill, 0)

    @pl.when(jnp.logical_not(has_left))
    def _():
        def fill(i, carry):
            left_in[i] = jnp.zeros((HALF, HALF), BF)
            return carry

        lax.fori_loop(0, PER, fill, 0)

    @pl.when(jnp.logical_not(has_right))
    def _():
        def fill(i, carry):
            right_in[i] = jnp.zeros((HALF, HALF), BF)
            return carry

        lax.fori_loop(0, PER, fill, 0)

    def clear_acc(w, carry):
        acc[w] = jnp.zeros((NB, NB), F32)
        return carry

    lax.fori_loop(0, W, clear_acc, 0)

    for c in range(STEPS):
        g_copy(c).wait()
    low_copy.wait()

    def correlate(s_base, green_ref, g_base):
        def one(t, carry):
            rows = pl.ds(pl.multiple_of(t * ROWS, ROWS), ROWS)
            held = [win[s_base + i, rows, :] for i in range(QUAD)]
            for w in range(W):
                at = g_base + shifts[w]
                terms = [held[i] * green_ref[at + i, rows, :] for i in range(QUAD)]
                acc[w, rows, :] += tree(terms).astype(F32)
            return carry

        lax.fori_loop(0, NB // ROWS, one, 0)

    a = grad[...]
    lc = left_cpl[...]
    rc = right_cpl[...]

    def step(at_step, carry):
        c = STEPS - 1 - at_step
        e0 = c * CH
        for i in range(CH):
            first[pl.ds(i * NB, NB), :] = nn(a, gown[e0 + i]).astype(BF)

        @pl.when(has_left)
        def _():
            left_copy(c).wait_recv()

        @pl.when(has_right)
        def _():
            right_copy(c).wait_recv()

        lp = [nn(lc, left_in[e0 + i]).astype(BF) for i in range(CH)]
        rp = [nn(rc, right_in[e0 + i]).astype(BF) for i in range(CH)]
        for i in range(CH):
            total = nt(first[pl.ds(i * NB, NB), :], a) + nt(lp[i], lc) + nt(rp[i], rc)
            win[PER + e0 + i] = total.astype(BF)

        needed = c >= SPLIT // CH
        aside = jnp.logical_and(me == crossing, jnp.logical_and(needed, relayed(c)))
        later = jnp.logical_and(me == crossing, jnp.logical_not(needed))

        @pl.when(jnp.logical_and(has_upper, jnp.logical_not(jnp.logical_or(aside, later))))
        def _():
            up_copy(c).start()

        @pl.when(aside)
        def _():
            aside_copy(c).start()

        @pl.when(has_right)
        def _():
            left_copy(c).wait_send()

        @pl.when(has_left)
        def _():
            right_copy(c).wait_send()

        @pl.when(at_step + AHEAD < STEPS)
        def _():
            start_surfaces(at_step + AHEAD)

        low = c + LAG
        pair = jnp.logical_and(low < STEPS, jnp.logical_and(low >= SPLIT // CH, lax.rem(at_step - LAG + 2 * STEPS, 2) == 1))

        @pl.when(pair)
        def _():
            @pl.when(has_lower)
            def _():
                up_copy(low + 1).wait_recv()
                up_copy(low).wait_recv()

            correlate(low * CH, glow, low * CH - SPLIT)

        @pl.when(at_step == STEPS // 2)
        def _():
            @pl.when(has_upper)
            def _():
                for p in range(4):
                    down_copy(p).wait_recv()

        @pl.when(jnp.logical_and(at_step >= STEPS // 2, c > 0))
        def _():
            top = PER - QUAD - (at_step - STEPS // 2) * QUAD
            correlate(PER + top, gown, top)

        before = jnp.minimum(c + 1, STEPS - 1)

        @pl.when(jnp.logical_and(
            jnp.logical_and(at_step > 0, before >= SPLIT // CH), jnp.logical_and(relayed(before), me == relay_of(before))))
        def _():
            aside_copy(before).wait_recv()
            relay_copy(before).start()

        for p in range(3):
            @pl.when(jnp.logical_and(at_step == 2, me == 14 - 2 * p))
            def _():
                down_aside(p).wait_recv()
                down_relay(p).start()

        return carry

    lax.fori_loop(0, STEPS, step, 0)

    for c in reversed(range(SPLIT // CH)):
        @pl.when(me == crossing)
        def _():
            (aside_copy(c) if c % 4 < 3 else up_copy(c)).start()

    def core_copy(j):
        return pltpu.make_async_remote_copy(
            src_ref=part.at[j], dst_ref=from_core.at[j], send_sem=c1s.at[j], recv_sem=c1r.at[j],
            device_id=partner, device_id_type=MESH)

    def finish(w, store):
        at = shifts[w]

        def one(t, carry):
            rows = pl.ds(pl.multiple_of(t * ROWS, ROWS), ROWS)
            terms = [win[PER + i, rows, :] * gown[at + i, rows, :] for i in range(QUAD)]
            store(rows, (acc[w, rows, :] + tree(terms).astype(F32)) * scale)
            return carry

        lax.fori_loop(0, NB // ROWS, one, 0)

    def theirs(k, carry):
        j = lax.rem(chip + k, CHIPS)

        def store(rows, value):
            part[j, rows, :] = value.astype(BF)

        finish(2 * j + 1 - core, store)
        core_copy(j).start()
        return carry

    lax.fori_loop(1, CHIPS + 1, theirs, 0)

    def ours(k, carry):
        j = lax.rem(chip + k, CHIPS)
        w = 2 * j + core

        def store(rows, value):
            acc[w, rows, :] = value

        finish(w, store)
        return carry

    lax.fori_loop(1, CHIPS + 1, ours, 0)

    def chip_copy(k):
        return pltpu.make_async_remote_copy(
            src_ref=sums.at[k - 1], dst_ref=from_chip.at[k - 1], send_sem=c2s.at[k - 1], recv_sem=c2r.at[k - 1],
            device_id={"energy": 2 * lax.rem(chip + k, CHIPS) + core, "layer": layer}, device_id_type=MESH)

    def join(k, carry):
        j = lax.rem(chip + k, CHIPS)
        w = 2 * j + core
        core_copy(j).wait_recv()

        def one(t, c2):
            rows = pl.ds(pl.multiple_of(t * ROWS, ROWS), ROWS)
            sums[k - 1, rows, :] = (acc[w, rows, :] + from_core[j, rows, :].astype(F32)).astype(BF)
            return c2

        lax.fori_loop(0, NB // ROWS, one, 0)
        chip_copy(k).start()
        return carry

    lax.fori_loop(1, CHIPS, join, 0)

    for c in reversed(range(SPLIT // CH)):
        if c % 4 < 3:
            @pl.when(me == relay_of(c))
            def _():
                aside_copy(c).wait_recv()
                relay_copy(c).start()

    core_copy(chip).wait_recv()
    for k in range(1, CHIPS):
        chip_copy(k).wait_recv()

    def total_rows(t, carry):
        rows = pl.ds(pl.multiple_of(t * ROWS, ROWS), ROWS)
        value = acc[me, rows, :] + from_core[chip, rows, :].astype(F32)
        for k in range(CHIPS - 1):
            value = value + from_chip[k, rows, :].astype(F32)
        self_out[rows, :] = value
        return carry

    lax.fori_loop(0, NB // ROWS, total_rows, 0)

    on_diag = lax.broadcasted_iota(jnp.int32, (NB, NB), 0) == lax.broadcasted_iota(jnp.int32, (NB, NB), 1)
    matrix = stiff[...] + COUPLING * self_out[...]
    matrix = matrix + jnp.where(on_diag, omega[me], 0.0)
    diag = jnp.where(on_diag, matrix, 0.0)
    inv_row = 1.0 / jnp.sum(diag, axis=0, keepdims=True)
    inv_col = 1.0 / jnp.sum(diag, axis=1, keepdims=True)
    approx = jnp.where(on_diag, 2.0 * inv_col, 0.0) - inv_col * (matrix * inv_row)
    matrix_halves = halves(matrix)
    for _ in range(NEWTON - 1):
        approx_halves = halves(approx)
        product = nn_split(matrix_halves, approx_halves)
        approx = 2.0 * approx - nn_split(approx_halves, halves(product))
    green_out[...] = approx
    rounded[me] = approx.astype(BF)

    row, column = lax.rem(chip, 4), chip // 4

    def chip_at(k):
        dx, dy = PLACES[k]
        return lax.rem(column + dx, 2) * 4 + lax.rem(row + dy, 4)

    def chip_from(k):
        dx, dy = PLACES[k]
        return lax.rem(column + dx, 2) * 4 + lax.rem(row + 4 - dy, 4)

    def gather_copy(k):
        return pltpu.make_async_remote_copy(
            src_ref=rounded.at[me], dst_ref=rounded.at[me], send_sem=gs.at[k - 1], recv_sem=gr.at[k - 1],
            device_id={"energy": 2 * chip_at(k) + core, "layer": layer}, device_id_type=MESH)

    def gather_arrival(k):
        w = 2 * chip_from(k) + core
        return pltpu.make_async_remote_copy(
            src_ref=rounded.at[w], dst_ref=rounded.at[w], send_sem=gs.at[k - 1], recv_sem=gr.at[k - 1],
            device_id={"energy": w, "layer": layer}, device_id_type=MESH)

    def pass_on(k, whose):
        w = 2 * chip_from(k) + whose
        return pltpu.make_async_remote_copy(
            src_ref=rounded.at[w], dst_ref=rounded.at[w], send_sem=fs.at[k], recv_sem=fr.at[k],
            device_id=partner, device_id_type=MESH)

    def turn_copy(t):
        rows = pl.ds(pl.multiple_of(t * ROWS, ROWS), ROWS)
        return pltpu.make_async_copy(mixture.at[:, rows, :], mixture_out.at[:, rows, :], ts.at[t])

    def add_group(pair, start, final):
        ws = []
        for k in pair:
            pass_on(k, 1 - core).wait_recv()
            ws += [2 * chip_from(k), 2 * chip_from(k) + 1]

        def mix_rows(t, carry):
            rows = pl.ds(pl.multiple_of(t * ROWS, ROWS), ROWS)
            held = [rounded[w, rows, :] for w in ws]
            ats = [PER - shifts[w] for w in ws]
            for e in range(PER):
                value = tree([held[i] * win[ats[i] + e, rows, :] for i in range(len(ws))]).astype(F32)
                if not start:
                    value = mix[e, rows, :] + value
                if final:
                    mixture[e, rows, :] = value.astype(BF)
                else:
                    mix[e, rows, :] = value
            if final:
                turn_copy(t).start()
            return carry

        lax.fori_loop(0, NB // ROWS, mix_rows, 0)

    pass_on(0, core).start()
    groups = [(0, 1), (2, 3), (4, 5), (6, 7)]
    for k in STAGES[0]:
        gather_copy(k).start()
    for c in range(SPLIT // CH):
        @pl.when(has_lower)
        def _():
            up_copy(c).wait_recv()

    ready = [0]
    for i, stage in enumerate(STAGES):
        for k in stage:
            gather_copy(k).wait_send()
        for k in STAGES[i + 1] if i + 1 < len(STAGES) else ():
            gather_copy(k).start()
        for k in stage:
            gather_arrival(k).wait_recv()
            pass_on(k, core).start()
        ready += stage
        while groups and all(k in ready for k in groups[0]):
            pair = groups.pop(0)
            add_group(pair, 0 in pair, not groups)

    for t in range(NB // ROWS):
        turn_copy(t).wait()
    for c in range(STEPS):
        @pl.when(has_upper)
        def _():
            up_copy(c).wait_send()

        if c % 4 < 3:
            @pl.when(me == relay_of(c))
            def _():
                relay_copy(c).wait_send()
    for p in range(4):
        @pl.when(has_lower)
        def _():
            down_copy(p).wait_send()

        if p < 3:
            @pl.when(me == 14 - 2 * p)
            def _():
                down_relay(p).wait_send()
    for j in range(CHIPS):
        core_copy(j).wait_send()
        pass_on(j, core).wait_send()
    for k in range(1, CHIPS):
        chip_copy(k).wait_send()


def last_kernel(grad, mixture, self_in, green_in, out, self_out, green_out, second):
    a = grad[...]
    for i in range(LAST):
        second[pl.ds(i * NB, NB), :] = nn(a, mixture[i]).astype(BF)
    out[...] = nt(second[...], a).astype(BF).reshape(LAST, NB, NB)
    self_out[...] = self_in[...]
    green_out[...] = green_in[...]


def body(green, gradient, left_coupling, right_coupling, dynamical, omega_sq, shifts):
    scale = 1.0 / math.sqrt(PER * lax.axis_size("energy"))
    vmem = pl.BlockSpec(memory_space=pltpu.VMEM)
    smem = pl.BlockSpec(memory_space=pltpu.SMEM)
    hbm = pl.BlockSpec(memory_space=pl.ANY)
    dma = pltpu.SemaphoreType.DMA
    own_self, own_green, mixture = pl.pallas_call(
        functools.partial(scatter_kernel, scale),
        out_shape=[
            jax.ShapeDtypeStruct((NB, NB), F32),
            jax.ShapeDtypeStruct((NB, NB), F32),
            jax.ShapeDtypeStruct((PER, NB, NB), BF),
        ],
        in_specs=[smem, smem, hbm, vmem, vmem, vmem, vmem],
        out_specs=[vmem, vmem, hbm],
        scratch_shapes=[
            pltpu.VMEM((2 * PER, NB, NB), BF),
            pltpu.VMEM((2 * PER - SPLIT, NB, NB), BF),
            pltpu.VMEM((2 * PER, NB, NB), BF),
            pltpu.VMEM((PER, HALF, HALF), BF),
            pltpu.VMEM((PER, HALF, HALF), BF),
            pltpu.VMEM((CH * NB, NB), BF),
            pltpu.VMEM((W, NB, NB), F32),
            pltpu.VMEM((CHIPS, NB, NB), BF),
            pltpu.VMEM((CHIPS - 1, NB, NB), BF),
            pltpu.VMEM((CHIPS, NB, NB), BF),
            pltpu.VMEM((CHIPS - 1, NB, NB), BF),
            pltpu.VMEM((W, NB, NB), BF),
            pltpu.VMEM((PER, NB, NB), F32),
            pltpu.VMEM((PER, NB, NB), BF),
            pltpu.VMEM((PER // 4, NB, NB), BF),
            pltpu.VMEM((DOWN, NB, NB), BF),
            dma((STEPS,)),
            dma((STEPS,)), dma((STEPS,)), dma((STEPS,)), dma((STEPS,)), dma((STEPS,)), dma((STEPS,)),
            dma((CHIPS,)), dma((CHIPS,)), dma((CHIPS - 1,)), dma((CHIPS - 1,)),
            dma((CHIPS - 1,)), dma((CHIPS - 1,)), dma((CHIPS,)), dma((CHIPS,)),
            dma((NB // ROWS,)), dma((STEPS // 4,)), dma((STEPS // 4,)),
            dma, dma((4,)), dma((4,)), dma, dma,
        ],
        compiler_params=pltpu.CompilerParams(
            collective_id=0, has_side_effects=True, vmem_limit_bytes=58 << 20),
        name="scatter",
    )(shifts, omega_sq, green[:, 0], gradient[0], left_coupling[0], right_coupling[0], dynamical[0])
    steps = PER // LAST
    block = pl.BlockSpec((LAST, NB, NB), lambda i: (i, 0, 0))
    whole = pl.BlockSpec((NB, NB), lambda i: (0, 0))
    piece = pl.BlockSpec((NB // steps, NB), lambda i: (i, 0))
    electron, own_self, own_green = pl.pallas_call(
        last_kernel,
        grid=(steps,),
        in_specs=[whole, block, piece, piece],
        out_specs=[block, piece, piece],
        out_shape=[
            jax.ShapeDtypeStruct((PER, NB, NB), BF),
            jax.ShapeDtypeStruct((NB, NB), F32),
            jax.ShapeDtypeStruct((NB, NB), F32),
        ],
        scratch_shapes=[pltpu.VMEM((LAST * NB, NB), BF)],
        compiler_params=pltpu.CompilerParams(vmem_limit_bytes=60 << 20),
        name="last",
    )(gradient[0], mixture, own_self, own_green)
    return own_self[None, None], own_green[None, None], electron[:, None]


def solution(mesh):
    return jax.shard_map(
        body,
        mesh=mesh,
        in_specs=(
            P("energy", "layer", None, None),
            P("layer", None, None),
            P("layer", None, None),
            P("layer", None, None),
            P("layer", None, None),
            P(),
            P(),
        ),
        out_specs=(
            P("energy", "layer", None, None),
            P("energy", "layer", None, None),
            P("energy", "layer", None, None),
        ),
        check_vma=False,
    )
```

```python
import functools
import math

import jax
import jax.numpy as jnp
from jax import lax
from jax.experimental import pallas as pl
from jax.experimental.pallas import tpu as pltpu
from jax.sharding import PartitionSpec as P

NEWTON = 3
COUPLING = 0.01
MESH = pl.DeviceIdType.MESH
BF = jnp.bfloat16
F32 = jnp.float32

PER = 32
NB = 256
HALF = 128
CH = 2
STEPS = PER // CH
AHEAD = 4
LAG = 4
W = 16
CHIPS = 8
PLACES = ((0, 0), (1, 0), (0, 1), (0, 3), (1, 1), (1, 3), (0, 2), (1, 2))
STAGES = [[1, 2, 3, 4, 5], [6, 7]]
LAST = 16
SPLIT = 16
QUAD = 4
DOWN = SPLIT // 4
ROWS = 32


def nn(a, b, **kw):
    return lax.dot_general(a, b, (((1,), (0,)), ((), ())), preferred_element_type=F32, **kw)


def nt(a, b, **kw):
    return lax.dot_general(a, b, (((1,), (1,)), ((), ())), preferred_element_type=F32, **kw)


def halves(a):
    high = a.astype(BF)
    return high, (a - high.astype(F32)).astype(BF)


def nn_split(a, b):
    return nn(a[0], b[0]) + (nn(a[0], b[1]) + nn(a[1], b[0]))


def tree(terms):
    while len(terms) > 1:
        terms = [terms[i] + terms[i + 1] if i + 1 < len(terms) else terms[i] for i in range(0, len(terms), 2)]
    return terms[0]


def scatter_kernel(
    scale, shifts, omega, green, grad, left_cpl, right_cpl, stiff,
    self_out, green_out, mixture_out,
    gown, glow, win, left_in, right_in, first, acc, part, sums, from_core, from_chip, rounded, mix, mixture, held_over, held_green,
    g_sem, ls, lr, rs, rr, us, ur, c1s, c1r, c2s, c2r, gs, gr, fs, fr, ts, hs, hr,
    low_sem, ds, dr, ks, kr,
):
    me = lax.axis_index("energy")
    layer = lax.axis_index("layer")
    core = lax.rem(me, 2)
    chip = me // 2
    has_lower, has_upper = me > 0, me < 15
    has_left, has_right = layer > 0, layer < 7
    partner = {"energy": me + 1 - 2 * core, "layer": layer}

    def g_copy(c):
        return pltpu.make_async_copy(
            green.at[pl.ds(c * CH, CH)], gown.at[pl.ds(c * CH, CH)], g_sem.at[c])

    def left_copy(c):
        return pltpu.make_async_remote_copy(
            src_ref=green.at[pl.ds(c * CH, CH), pl.ds(HALF, HALF), pl.ds(HALF, HALF)],
            dst_ref=left_in.at[pl.ds(c * CH, CH)], send_sem=ls.at[c], recv_sem=lr.at[c],
            device_id={"energy": me, "layer": lax.rem(layer + 1, 8)}, device_id_type=MESH)

    def right_copy(c):
        return pltpu.make_async_remote_copy(
            src_ref=green.at[pl.ds(c * CH, CH), pl.ds(0, HALF), pl.ds(0, HALF)],
            dst_ref=right_in.at[pl.ds(c * CH, CH)], send_sem=rs.at[c], recv_sem=rr.at[c],
            device_id={"energy": me, "layer": lax.rem(layer + 7, 8)}, device_id_type=MESH)

    def up_copy(c):
        return pltpu.make_async_remote_copy(
            src_ref=win.at[pl.ds(PER + c * CH, CH)], dst_ref=win.at[pl.ds(c * CH, CH)],
            send_sem=us.at[c], recv_sem=ur.at[c],
            device_id={"energy": lax.rem(me + 1, 16), "layer": layer}, device_id_type=MESH)

    crossing = 7

    def relay_of(c):
        return lax.rem(4 * lax.rem(c, 4), 6)

    def relayed(c):
        return lax.rem(c, 4) < 3

    def aside_copy(c):
        return pltpu.make_async_remote_copy(
            src_ref=win.at[pl.ds(PER + c * CH, CH)], dst_ref=held_over.at[pl.ds(c // 4 * CH, CH)],
            send_sem=us.at[c], recv_sem=hr.at[c // 4],
            device_id={"energy": relay_of(c), "layer": layer}, device_id_type=MESH)

    def relay_copy(c):
        return pltpu.make_async_remote_copy(
            src_ref=held_over.at[pl.ds(c // 4 * CH, CH)], dst_ref=win.at[pl.ds(c * CH, CH)],
            send_sem=hs.at[c // 4], recv_sem=ur.at[c],
            device_id={"energy": crossing + 1, "layer": layer}, device_id_type=MESH)

    def down_copy(p):
        return pltpu.make_async_remote_copy(
            src_ref=green.at[pl.ds(p * DOWN, DOWN)], dst_ref=gown.at[pl.ds(PER + p * DOWN, DOWN)],
            send_sem=ds.at[p], recv_sem=dr.at[p],
            device_id={"energy": lax.rem(me + 15, 16), "layer": layer}, device_id_type=MESH)

    def down_aside(p):
        return pltpu.make_async_remote_copy(
            src_ref=green.at[pl.ds(p * DOWN, DOWN)], dst_ref=held_green, send_sem=ds.at[p], recv_sem=kr,
            device_id={"energy": 14 - 2 * p, "layer": layer}, device_id_type=MESH)

    def down_relay(p):
        return pltpu.make_async_remote_copy(
            src_ref=held_green, dst_ref=gown.at[pl.ds(PER + p * DOWN, DOWN)], send_sem=ks, recv_sem=dr.at[p],
            device_id={"energy": crossing, "layer": layer}, device_id_type=MESH)

    low_copy = pltpu.make_async_copy(green.at[pl.ds(SPLIT, PER - SPLIT)], glow.at[pl.ds(PER, PER - SPLIT)], low_sem)

    def start_surfaces(step):
        c = STEPS - 1 - step
        @pl.when(has_right)
        def _():
            left_copy(c).start()

        @pl.when(has_left)
        def _():
            right_copy(c).start()

    for c in reversed(range(STEPS)):
        g_copy(c).start()
    low_copy.start()

    barrier = pltpu.get_barrier_semaphore()
    for k in range(1, 16):
        pl.semaphore_signal(
            barrier, inc=1, device_id={"energy": lax.rem(me + k, 16), "layer": layer}, device_id_type=MESH)

    @pl.when(has_right)
    def _():
        pl.semaphore_signal(barrier, inc=1, device_id={"energy": me, "layer": layer + 1}, device_id_type=MESH)

    @pl.when(has_left)
    def _():
        pl.semaphore_signal(barrier, inc=1, device_id={"energy": me, "layer": layer - 1}, device_id_type=MESH)

    pl.semaphore_wait(barrier, 15 + has_left.astype(jnp.int32) + has_right.astype(jnp.int32))

    for c in range(AHEAD):
        start_surfaces(c)

    for p in range(4):
        split_path = me == crossing + 1 if p < 3 else me < 0

        @pl.when(jnp.logical_and(has_lower, jnp.logical_not(split_path)))
        def _():
            down_copy(p).start()

        @pl.when(split_path)
        def _():
            down_aside(p).start()

    def clear(i, carry):
        zero = jnp.zeros((NB, NB), BF)
        glow[i] = zero
        return carry

    lax.fori_loop(0, PER, clear, 0)

    def clear_top(i, carry):
        gown[i] = jnp.zeros((NB, NB), BF)
        return carry

    lax.fori_loop(PER + SPLIT, 2 * PER, clear_top, 0)

    @pl.when(jnp.logical_not(has_upper))
    def _():
        lax.fori_loop(PER, PER + SPLIT, clear_top, 0)

    @pl.when(jnp.logical_not(has_lower))
    def _():
        def fill(i, carry):
            win[i] = jnp.zeros((NB, NB), BF)
            return carry

        lax.fori_loop(0, PER, fill, 0)

    @pl.when(jnp.logical_not(has_left))
    def _():
        def fill(i, carry):
            left_in[i] = jnp.zeros((HALF, HALF), BF)
            return carry

        lax.fori_loop(0, PER, fill, 0)

    @pl.when(jnp.logical_not(has_right))
    def _():
        def fill(i, carry):
            right_in[i] = jnp.zeros((HALF, HALF), BF)
            return carry

        lax.fori_loop(0, PER, fill, 0)

    def clear_acc(w, carry):
        acc[w] = jnp.zeros((NB, NB), F32)
        return carry

    lax.fori_loop(0, W, clear_acc, 0)

    for c in range(STEPS):
        g_copy(c).wait()
    low_copy.wait()

    def correlate(s_base, green_ref, g_base):
        def one(t, carry):
            rows = pl.ds(pl.multiple_of(t * ROWS, ROWS), ROWS)
            held = [win[s_base + i, rows, :] for i in range(QUAD)]
            for w in range(W):
                at = g_base + shifts[w]
                terms = [held[i] * green_ref[at + i, rows, :] for i in range(QUAD)]
                acc[w, rows, :] += tree(terms).astype(F32)
            return carry

        lax.fori_loop(0, NB // ROWS, one, 0)

    a = grad[...]
    lc = left_cpl[...]
    rc = right_cpl[...]

    def step(at_step, carry):
        c = STEPS - 1 - at_step
        e0 = c * CH
        for i in range(CH):
            first[pl.ds(i * NB, NB), :] = nn(a, gown[e0 + i]).astype(BF)

        @pl.when(has_left)
        def _():
            left_copy(c).wait_recv()

        @pl.when(has_right)
        def _():
            right_copy(c).wait_recv()

        lp = [nn(lc, left_in[e0 + i]).astype(BF) for i in range(CH)]
        rp = [nn(rc, right_in[e0 + i]).astype(BF) for i in range(CH)]
        for i in range(CH):
            total = nt(first[pl.ds(i * NB, NB), :], a) + nt(lp[i], lc) + nt(rp[i], rc)
            win[PER + e0 + i] = total.astype(BF)

        needed = c >= SPLIT // CH
        aside = jnp.logical_and(me == crossing, jnp.logical_and(needed, relayed(c)))
        later = jnp.logical_and(me == crossing, jnp.logical_not(needed))

        @pl.when(jnp.logical_and(has_upper, jnp.logical_not(jnp.logical_or(aside, later))))
        def _():
            up_copy(c).start()

        @pl.when(aside)
        def _():
            aside_copy(c).start()

        @pl.when(has_right)
        def _():
            left_copy(c).wait_send()

        @pl.when(has_left)
        def _():
            right_copy(c).wait_send()

        @pl.when(at_step + AHEAD < STEPS)
        def _():
            start_surfaces(at_step + AHEAD)

        low = c + LAG
        pair = jnp.logical_and(low < STEPS, jnp.logical_and(low >= SPLIT // CH, lax.rem(at_step - LAG + 2 * STEPS, 2) == 1))

        @pl.when(pair)
        def _():
            @pl.when(has_lower)
            def _():
                up_copy(low + 1).wait_recv()
                up_copy(low).wait_recv()

            correlate(low * CH, glow, low * CH - SPLIT)

        @pl.when(at_step == STEPS // 2)
        def _():
            @pl.when(has_upper)
            def _():
                for p in range(4):
                    down_copy(p).wait_recv()

        @pl.when(jnp.logical_and(at_step >= STEPS // 2, c > 0))
        def _():
            top = PER - QUAD - (at_step - STEPS // 2) * QUAD
            correlate(PER + top, gown, top)

        before = jnp.minimum(c + 1, STEPS - 1)

        @pl.when(jnp.logical_and(
            jnp.logical_and(at_step > 0, before >= SPLIT // CH), jnp.logical_and(relayed(before), me == relay_of(before))))
        def _():
            aside_copy(before).wait_recv()
            relay_copy(before).start()

        for p in range(3):
            @pl.when(jnp.logical_and(at_step == 2, me == 14 - 2 * p))
            def _():
                down_aside(p).wait_recv()
                down_relay(p).start()

        return carry

    lax.fori_loop(0, STEPS, step, 0)

    for c in reversed(range(SPLIT // CH)):
        @pl.when(me == crossing)
        def _():
            (aside_copy(c) if c % 4 < 3 else up_copy(c)).start()

    def core_copy(j):
        return pltpu.make_async_remote_copy(
            src_ref=part.at[j], dst_ref=from_core.at[j], send_sem=c1s.at[j], recv_sem=c1r.at[j],
            device_id=partner, device_id_type=MESH)

    def finish(w, store):
        at = shifts[w]

        def one(t, carry):
            rows = pl.ds(pl.multiple_of(t * ROWS, ROWS), ROWS)
            terms = [win[PER + i, rows, :] * gown[at + i, rows, :] for i in range(QUAD)]
            store(rows, (acc[w, rows, :] + tree(terms).astype(F32)) * scale)
            return carry

        lax.fori_loop(0, NB // ROWS, one, 0)

    def theirs(k, carry):
        j = lax.rem(chip + k, CHIPS)

        def store(rows, value):
            part[j, rows, :] = value.astype(BF)

        finish(2 * j + 1 - core, store)
        core_copy(j).start()
        return carry

    lax.fori_loop(1, CHIPS + 1, theirs, 0)

    def ours(k, carry):
        j = lax.rem(chip + k, CHIPS)
        w = 2 * j + core

        def store(rows, value):
            acc[w, rows, :] = value

        finish(w, store)
        return carry

    lax.fori_loop(1, CHIPS + 1, ours, 0)

    def chip_copy(k):
        return pltpu.make_async_remote_copy(
            src_ref=sums.at[k - 1], dst_ref=from_chip.at[k - 1], send_sem=c2s.at[k - 1], recv_sem=c2r.at[k - 1],
            device_id={"energy": 2 * lax.rem(chip + k, CHIPS) + core, "layer": layer}, device_id_type=MESH)

    def join(k, carry):
        j = lax.rem(chip + k, CHIPS)
        w = 2 * j + core
        core_copy(j).wait_recv()

        def one(t, c2):
            rows = pl.ds(pl.multiple_of(t * ROWS, ROWS), ROWS)
            sums[k - 1, rows, :] = (acc[w, rows, :] + from_core[j, rows, :].astype(F32)).astype(BF)
            return c2

        lax.fori_loop(0, NB // ROWS, one, 0)
        chip_copy(k).start()
        return carry

    lax.fori_loop(1, CHIPS, join, 0)

    for c in reversed(range(SPLIT // CH)):
        if c % 4 < 3:
            @pl.when(me == relay_of(c))
            def _():
                aside_copy(c).wait_recv()
                relay_copy(c).start()

    core_copy(chip).wait_recv()
    for k in range(1, CHIPS):
        chip_copy(k).wait_recv()

    def total_rows(t, carry):
        rows = pl.ds(pl.multiple_of(t * ROWS, ROWS), ROWS)
        value = acc[me, rows, :] + from_core[chip, rows, :].astype(F32)
        for k in range(CHIPS - 1):
            value = value + from_chip[k, rows, :].astype(F32)
        self_out[rows, :] = value
        return carry

    lax.fori_loop(0, NB // ROWS, total_rows, 0)

    on_diag = lax.broadcasted_iota(jnp.int32, (NB, NB), 0) == lax.broadcasted_iota(jnp.int32, (NB, NB), 1)
    matrix = stiff[...] + COUPLING * self_out[...]
    matrix = matrix + jnp.where(on_diag, omega[me], 0.0)
    diag = jnp.where(on_diag, matrix, 0.0)
    inv_row = 1.0 / jnp.sum(diag, axis=0, keepdims=True)
    inv_col = 1.0 / jnp.sum(diag, axis=1, keepdims=True)
    approx = jnp.where(on_diag, 2.0 * inv_col, 0.0) - inv_col * (matrix * inv_row)
    matrix_halves = halves(matrix)
    for _ in range(NEWTON - 1):
        approx_halves = halves(approx)
        product = nn_split(matrix_halves, approx_halves)
        approx = 2.0 * approx - nn_split(approx_halves, halves(product))
    green_out[...] = approx
    rounded[me] = approx.astype(BF)

    row, column = lax.rem(chip, 4), chip // 4

    def chip_at(k):
        dx, dy = PLACES[k]
        return lax.rem(column + dx, 2) * 4 + lax.rem(row + dy, 4)

    def chip_from(k):
        dx, dy = PLACES[k]
        return lax.rem(column + dx, 2) * 4 + lax.rem(row + 4 - dy, 4)

    def gather_copy(k):
        return pltpu.make_async_remote_copy(
            src_ref=rounded.at[me], dst_ref=rounded.at[me], send_sem=gs.at[k - 1], recv_sem=gr.at[k - 1],
            device_id={"energy": 2 * chip_at(k) + core, "layer": layer}, device_id_type=MESH)

    def gather_arrival(k):
        w = 2 * chip_from(k) + core
        return pltpu.make_async_remote_copy(
            src_ref=rounded.at[w], dst_ref=rounded.at[w], send_sem=gs.at[k - 1], recv_sem=gr.at[k - 1],
            device_id={"energy": w, "layer": layer}, device_id_type=MESH)

    def pass_on(k, whose):
        w = 2 * chip_from(k) + whose
        return pltpu.make_async_remote_copy(
            src_ref=rounded.at[w], dst_ref=rounded.at[w], send_sem=fs.at[k], recv_sem=fr.at[k],
            device_id=partner, device_id_type=MESH)

    def turn_copy(t):
        rows = pl.ds(pl.multiple_of(t * ROWS, ROWS), ROWS)
        return pltpu.make_async_copy(mixture.at[:, rows, :], mixture_out.at[:, rows, :], ts.at[t])

    def add_group(pair, start, final):
        ws = []
        for k in pair:
            pass_on(k, 1 - core).wait_recv()
            ws += [2 * chip_from(k), 2 * chip_from(k) + 1]

        def mix_rows(t, carry):
            rows = pl.ds(pl.multiple_of(t * ROWS, ROWS), ROWS)
            held = [rounded[w, rows, :] for w in ws]
            ats = [PER - shifts[w] for w in ws]
            for e in range(PER):
                value = tree([held[i] * win[ats[i] + e, rows, :] for i in range(len(ws))]).astype(F32)
                if not start:
                    value = mix[e, rows, :] + value
                if final:
                    mixture[e, rows, :] = value.astype(BF)
                else:
                    mix[e, rows, :] = value
            if final:
                turn_copy(t).start()
            return carry

        lax.fori_loop(0, NB // ROWS, mix_rows, 0)

    pass_on(0, core).start()
    groups = [(0, 1), (2, 3), (4, 5), (6, 7)]
    for k in STAGES[0]:
        gather_copy(k).start()
    ready = [0]
    for i, stage in enumerate(STAGES):
        for k in stage:
            gather_copy(k).wait_send()
        for k in STAGES[i + 1] if i + 1 < len(STAGES) else ():
            gather_copy(k).start()
        for k in stage:
            gather_arrival(k).wait_recv()
            pass_on(k, core).start()
        for c in range(SPLIT // CH if i == 0 else 0):
            @pl.when(has_lower)
            def _():
                up_copy(c).wait_recv()

        ready += stage
        while groups and all(k in ready for k in groups[0]):
            pair = groups.pop(0)
            add_group(pair, 0 in pair, not groups)

    for t in range(NB // ROWS):
        turn_copy(t).wait()
    for c in range(STEPS):
        @pl.when(has_upper)
        def _():
            up_copy(c).wait_send()

        if c % 4 < 3:
            @pl.when(me == relay_of(c))
            def _():
                relay_copy(c).wait_send()
    for p in range(4):
        @pl.when(has_lower)
        def _():
            down_copy(p).wait_send()

        if p < 3:
            @pl.when(me == 14 - 2 * p)
            def _():
                down_relay(p).wait_send()
    for j in range(CHIPS):
        core_copy(j).wait_send()
        pass_on(j, core).wait_send()
    for k in range(1, CHIPS):
        chip_copy(k).wait_send()


def last_kernel(grad, mixture, self_in, green_in, out, self_out, green_out, second):
    a = grad[...]
    for i in range(LAST):
        second[pl.ds(i * NB, NB), :] = nn(a, mixture[i]).astype(BF)
    out[...] = nt(second[...], a).astype(BF).reshape(LAST, NB, NB)
    self_out[...] = self_in[...]
    green_out[...] = green_in[...]


def body(green, gradient, left_coupling, right_coupling, dynamical, omega_sq, shifts):
    scale = 1.0 / math.sqrt(PER * lax.axis_size("energy"))
    vmem = pl.BlockSpec(memory_space=pltpu.VMEM)
    smem = pl.BlockSpec(memory_space=pltpu.SMEM)
    hbm = pl.BlockSpec(memory_space=pl.ANY)
    dma = pltpu.SemaphoreType.DMA
    own_self, own_green, mixture = pl.pallas_call(
        functools.partial(scatter_kernel, scale),
        out_shape=[
            jax.ShapeDtypeStruct((NB, NB), F32),
            jax.ShapeDtypeStruct((NB, NB), F32),
            jax.ShapeDtypeStruct((PER, NB, NB), BF),
        ],
        in_specs=[smem, smem, hbm, vmem, vmem, vmem, vmem],
        out_specs=[vmem, vmem, hbm],
        scratch_shapes=[
            pltpu.VMEM((2 * PER, NB, NB), BF),
            pltpu.VMEM((2 * PER - SPLIT, NB, NB), BF),
            pltpu.VMEM((2 * PER, NB, NB), BF),
            pltpu.VMEM((PER, HALF, HALF), BF),
            pltpu.VMEM((PER, HALF, HALF), BF),
            pltpu.VMEM((CH * NB, NB), BF),
            pltpu.VMEM((W, NB, NB), F32),
            pltpu.VMEM((CHIPS, NB, NB), BF),
            pltpu.VMEM((CHIPS - 1, NB, NB), BF),
            pltpu.VMEM((CHIPS, NB, NB), BF),
            pltpu.VMEM((CHIPS - 1, NB, NB), BF),
            pltpu.VMEM((W, NB, NB), BF),
            pltpu.VMEM((PER, NB, NB), F32),
            pltpu.VMEM((PER, NB, NB), BF),
            pltpu.VMEM((PER // 4, NB, NB), BF),
            pltpu.VMEM((DOWN, NB, NB), BF),
            dma((STEPS,)),
            dma((STEPS,)), dma((STEPS,)), dma((STEPS,)), dma((STEPS,)), dma((STEPS,)), dma((STEPS,)),
            dma((CHIPS,)), dma((CHIPS,)), dma((CHIPS - 1,)), dma((CHIPS - 1,)),
            dma((CHIPS - 1,)), dma((CHIPS - 1,)), dma((CHIPS,)), dma((CHIPS,)),
            dma((NB // ROWS,)), dma((STEPS // 4,)), dma((STEPS // 4,)),
            dma, dma((4,)), dma((4,)), dma, dma,
        ],
        compiler_params=pltpu.CompilerParams(
            collective_id=0, has_side_effects=True, vmem_limit_bytes=58 << 20),
        name="scatter",
    )(shifts, omega_sq, green[:, 0], gradient[0], left_coupling[0], right_coupling[0], dynamical[0])
    steps = PER // LAST
    block = pl.BlockSpec((LAST, NB, NB), lambda i: (i, 0, 0))
    whole = pl.BlockSpec((NB, NB), lambda i: (0, 0))
    piece = pl.BlockSpec((NB // steps, NB), lambda i: (i, 0))
    electron, own_self, own_green = pl.pallas_call(
        last_kernel,
        grid=(steps,),
        in_specs=[whole, block, piece, piece],
        out_specs=[block, piece, piece],
        out_shape=[
            jax.ShapeDtypeStruct((PER, NB, NB), BF),
            jax.ShapeDtypeStruct((NB, NB), F32),
            jax.ShapeDtypeStruct((NB, NB), F32),
        ],
        scratch_shapes=[pltpu.VMEM((LAST * NB, NB), BF)],
        compiler_params=pltpu.CompilerParams(vmem_limit_bytes=60 << 20),
        name="last",
    )(gradient[0], mixture, own_self, own_green)
    return own_self[None, None], own_green[None, None], electron[:, None]


def solution(mesh):
    return jax.shard_map(
        body,
        mesh=mesh,
        in_specs=(
            P("energy", "layer", None, None),
            P("layer", None, None),
            P("layer", None, None),
            P("layer", None, None),
            P("layer", None, None),
            P(),
            P(),
        ),
        out_specs=(
            P("energy", "layer", None, None),
            P("energy", "layer", None, None),
            P("energy", "layer", None, None),
        ),
        check_vma=False,
    )
```
